128 devices in a mesh: section: 2 (over z_lo), dp: 16 (over y, z_hi, core), fsdp: 4 (over x).
Axes of the slice: x: 4, y: 4, z: 4 (z_hi: 2, z_lo: 2; z = z_hi * 2 + z_lo), core: 2. Of those that a mesh axis runs over, the one named last changes fastest.
Arguments:
- inputs: bfloat16 [2, 8192, 1024], P(None, ('dp', 'fsdp')), may hold values from -6 to 6
- cotangent: bfloat16 [2, 8192, 1024], P(None, ('dp', 'fsdp')), may hold values from -6 to 6
- lengths: int32 [2, 64, 4], P(None, ('dp', 'fsdp')), may hold values from 1 to 64, 128 in all within a row
- expert_ids: int32 [2, 2, 8192, 4], P('section', None, ('dp', 'fsdp')), may hold values from 0 to 7, all different within a row; in each aligned block of 128 rows (0 to 127, 128 to 255, ..., all dimensions but the last counted through in order) at most 80 rows name the same one
- gain_attn: bfloat16 [2, 1024], P('section', 'fsdp'), may hold values from 0.5 to 1.5
- w_query: bfloat16 [2, 1024, 1024], P('section', 'fsdp'), may hold values from -0.1875 to 0.1875
- w_key: bfloat16 [2, 1024, 512], P('section', 'fsdp'), may hold values from -0.1875 to 0.1875
- w_value: bfloat16 [2, 1024, 512], P('section', 'fsdp'), may hold values from -0.1875 to 0.1875
- w_out: bfloat16 [2, 1024, 1024], P('section', 'fsdp'), may hold values from -0.75 to 0.75
- gain_ffn: bfloat16 [2, 1024], P('section', 'fsdp'), may hold values from 0.5 to 1.5
- w_router: bfloat16 [2, 1024, 8], P('section', 'fsdp'), may hold values from -0.09375 to 0.09375
- w_gate: bfloat16 [2, 1024, 8, 512], P('section', 'fsdp'), may hold values from -0.1875 to 0.1875
- w_up: bfloat16 [2, 1024, 8, 512], P('section', 'fsdp'), may hold values from -0.1875 to 0.1875
- w_down: bfloat16 [2, 8, 512, 1024], P('section', None, None, 'fsdp'), may hold values from -1 to 1
Outputs:
- layer_outputs: bfloat16 [2, 2, 8192, 1024], P('section', None, ('dp', 'fsdp'))
- input_grads: bfloat16 [2, 2, 8192, 1024], P('section', None, ('dp', 'fsdp'))
- grad_gain_attn: float32 [2, 1024], P('section', 'fsdp')
- grad_query: float32 [2, 1024, 1024], P('section', 'fsdp')
- grad_key: float32 [2, 1024, 512], P('section', 'fsdp')
- grad_value: float32 [2, 1024, 512], P('section', 'fsdp')
- grad_out: float32 [2, 1024, 1024], P('section', 'fsdp')
- grad_gain_ffn: float32 [2, 1024], P('section', 'fsdp')
- grad_router: float32 [2, 1024, 8], P('section', 'fsdp')
- grad_gate: float32 [2, 1024, 8, 512], P('section', 'fsdp')
- grad_up: float32 [2, 1024, 8, 512], P('section', 'fsdp')
- grad_down: float32 [2, 8, 512, 1024], P('section', None, None, 'fsdp')
The draws below stay inside these ranges and needn't reach their ends.
Inputs may be any that keep to these rules, and one draw needn't show every extreme that they name: In each row the 4 lengths sum to 128, and the longest is exactly 64. `expert_ids`: each token names 4 different experts. Among the 128 tokens of one row for one layer (aligned blocks of 128 rows), no expert is named by more than 80 tokens, and in every draw some block has an expert named by exactly 80.
All inputs are finite; a program needn't handle non-finite values.
Results may differ from the reference program's by a relative error of at most 0.03.
Values may be sent and summed in bfloat16 or wider, within the bound.
No kernel may reach another device: no remote copies, remote signals or barrier semaphores. Data moves between devices by JAX's collectives and lax.ppermute only.
A program may use at most 256 MiB of HBM per device.

```python
import math
import jax
import jax.numpy as jnp
import numpy as np
from jax import lax

D = 1024
HEADS = 16
KV_HEADS = 8
HEAD_DIM = 64
FF = 512
EXPERTS = 8
TOP = 4
MICRO = 2
NSEQ = 4
TOK_DEV = 128
SEQ_MOST = 64
CAP = 80
ROWS = 64
TOKENS = 8192
N_SECTION = 2
N_DP = 16
N_FSDP = 4


def block_scale(stream_key, dims, shards, low, largest):
    level = 1.0
    for dim, blocks in shards:
        steps = jax.random.uniform(jax.random.fold_in(jax.random.fold_in(stream_key, 6), dim), (blocks,), jnp.float32, low / len(shards), largest / len(shards))
        level = level * jnp.repeat(jnp.exp(steps), dims[dim] // blocks).reshape((-1,) + (1,) * (len(dims) - 1 - dim))
    return level


def length_profile(amount, total, limit, lean):
    weights = [(1 << 20) // math.isqrt(standing ** lean) + 1 for standing in range(2, amount + 1)]
    surplus, given = total - limit - (amount - 1), [1] * (amount - 1)
    while surplus > 0:
        free = [i for i in range(amount - 1) if given[i] < limit]
        pool, budget = sum([weights[i] for i in free]), surplus
        for i in free:
            more = min(limit - given[i], max(1, budget * weights[i] // pool), surplus)
            given[i] = given[i] + more
            surplus = surplus - more
    return np.array([limit] + given)


def ragged(key, amount, total, most, lean):
    if amount == 2:
        one = jax.random.randint(key, (), max(1, total - most), min(most, total - 1) + 1)
        return jnp.stack([one, total - one])
    tallies = jnp.asarray(length_profile(amount, total, most, lean), jnp.int32)
    couples = (amount - 1) // 2
    source_of, receiver = tallies[1:1 + 2 * couples:2], tallies[2:2 + 2 * couples:2]
    margin = jnp.minimum(source_of - 1, most - receiver)
    passed = jax.random.randint(jax.random.fold_in(key, 1), (couples,), 0, 1 << 20) % (margin + 1)
    tallies = tallies.at[1:1 + 2 * couples:2].set(source_of - passed).at[2:2 + 2 * couples:2].set(receiver + passed)
    return tallies[jax.random.permutation(jax.random.fold_in(key, 2), amount)]


def routed_block(own_key, own, number, rows, amount, top, limit, slope):
    order = jax.random.permutation(own_key, amount)
    heavy_load, ordinary = load_shares(amount, rows * top, limit, slope, True), load_shares(amount, rows * top, limit, slope, False)
    places = jnp.arange(amount)

    def named(sizes, rotation):
        used = int((sizes > 0).sum())
        fixed = max(1, used // 4)
        passed = fixed + (places - fixed + rotation * (used - fixed)) % max(1, amount - fixed)
        return jnp.zeros((amount,), jnp.int32).at[order[jnp.where(places < fixed, places, passed)]].set(jnp.asarray(sizes, jnp.int32))

    sizes = jnp.where(number % 4 == 0, named(heavy_load, number // 4), named(ordinary, number - number // 4 - 1))
    mixed = jax.random.permutation(jax.random.fold_in(own, 3), amount)
    giver, sink = mixed[0:amount // 2 * 2:2], mixed[1:amount // 2 * 2:2]
    margin = jnp.minimum(sizes[giver] - 1, limit - sizes[sink]) // 2
    margin = jnp.where((giver == order[0]) | (sink == order[0]) | (sizes[sink] == 0), 0, jnp.maximum(margin, 0))
    passed = jax.random.randint(jax.random.fold_in(own, 4), (amount // 2,), 0, 1 << 20) % (margin + 1)
    sizes = sizes.at[giver].add(-passed).at[sink].add(passed)
    labels = jnp.searchsorted(jnp.cumsum(sizes), jnp.arange(rows * top), side="right").astype(jnp.int32)
    grid = labels.reshape(top, rows).T
    grid = grid[jax.random.permutation(jax.random.fold_in(own, 1), rows)]
    rotation = jax.random.randint(jax.random.fold_in(own, 2), (rows, 1), 0, top)
    return jnp.take_along_axis(grid, (jnp.arange(top)[None, :] + rotation) % top, axis=1)


def load_shares(count, total, most, slope, full):
    loads = [(1 << 20) // math.isqrt(standing ** slope) + 1 for standing in range(1, count + 1)]
    largest = most if full else min(most, max(-(-total // count), total * loads[0] // sum(loads)))
    least = 1 if total - largest >= count - 1 else 0
    counts, surplus = [largest] + [least] * (count - 1), total - largest - least * (count - 1)
    while surplus > 0:
        movable = [i for i in range(1, count) if counts[i] < largest] or [i for i in range(1, count) if counts[i] < most]
        whole, remaining = sum([loads[i] for i in movable]), surplus
        for i in movable:
            addition = min(most - counts[i], max(1, remaining * loads[i] // whole), surplus)
            counts[i] = counts[i] + addition
            surplus = surplus - addition
    return np.array(counts)


def bell_draw(own_key, shape, spread, limit, pieces=(), kind=jnp.bfloat16):
    entries = jax.random.normal(own_key, shape, jnp.float32) * spread
    if len(pieces) > 0:
        entries = block_scale(own_key, shape, pieces, -0.22, 0.18) * entries
    return jnp.clip(entries, min=-limit, max=limit).astype(kind)


def setup_inputs(seed: int = 0) -> dict:
    splits = jax.random.split(jax.random.key(seed), 15)
    inputs = bell_draw(splits[0], (MICRO, TOKENS, D), 1.0, 6.0, ((1, 64),))
    cotangent = bell_draw(splits[1], (MICRO, TOKENS, D), 1.0, 6.0, ((1, 64),))
    lengths = jax.vmap(lambda own: ragged(own, NSEQ, TOK_DEV, SEQ_MOST, 1))(jax.random.split(splits[2], MICRO * ROWS)).reshape((MICRO, ROWS, NSEQ)).astype(jnp.int32)
    expert_ids_keys = jax.random.split(jax.random.fold_in(splits[3], 1), N_SECTION * MICRO * TOKENS // TOK_DEV)
    expert_ids_turns = jax.random.permutation(jax.random.fold_in(splits[3], 3), N_SECTION * MICRO * TOKENS // TOK_DEV)
    expert_ids = jax.vmap(lambda own, number: routed_block(jax.random.fold_in(splits[3], 2), own, number, TOK_DEV, EXPERTS, TOP, CAP, 2))(expert_ids_keys, expert_ids_turns).reshape((N_SECTION, MICRO, TOKENS, TOP))
    gain_attn = jnp.clip(1.0 + 0.1 * jax.random.normal(splits[4], (N_SECTION, D), jnp.float32), 0.5, 1.5).astype(jnp.bfloat16)
    w_query = bell_draw(splits[5], (N_SECTION, D, HEADS * HEAD_DIM), D ** -0.5, 0.1875, ((0, 2), (1, 4)))
    w_key = bell_draw(splits[6], (N_SECTION, D, KV_HEADS * HEAD_DIM), D ** -0.5, 0.1875, ((0, 2), (1, 4)))
    w_value = bell_draw(splits[7], (N_SECTION, D, KV_HEADS * HEAD_DIM), D ** -0.5, 0.1875, ((0, 2), (1, 4)))
    w_out = bell_draw(splits[8], (N_SECTION, HEADS * HEAD_DIM, D), (HEADS * HEAD_DIM // 16) ** -0.5, 0.75, ((0, 2), (1, 4)))
    gain_ffn = jnp.clip(1.0 + 0.1 * jax.random.normal(splits[9], (N_SECTION, D), jnp.float32), 0.5, 1.5).astype(jnp.bfloat16)
    w_router = bell_draw(splits[10], (N_SECTION, D, EXPERTS), (4 * D) ** -0.5, 0.09375, ((0, 2), (1, 4)))
    w_gate = bell_draw(splits[11], (N_SECTION, D, EXPERTS, FF), D ** -0.5, 0.1875, ((0, 2), (1, 4)))
    w_up = bell_draw(splits[12], (N_SECTION, D, EXPERTS, FF), D ** -0.5, 0.1875, ((0, 2), (1, 4)))
    w_down = bell_draw(splits[13], (N_SECTION, EXPERTS, FF, D), (FF // 16) ** -0.5, 1.0, ((0, 2), (3, 4)))
    return dict(inputs=inputs, cotangent=cotangent, lengths=lengths, expert_ids=expert_ids, gain_attn=gain_attn, w_query=w_query, w_key=w_key, w_value=w_value, w_out=w_out, gain_ffn=gain_ffn, w_router=w_router, w_gate=w_gate, w_up=w_up, w_down=w_down)


@jax.custom_vjp
def low(v):
    return lax.optimization_barrier(v.astype(jnp.bfloat16)).astype(jnp.float32)

@jax.custom_vjp
def low_back(v):
    return v

def low_keep(v):
    return (low(v), None)

def low_pass(kept, grad):
    return (grad,)

def back_keep(v):
    return (v, None)

def back_low(kept, grad):
    return (low(grad),)
low.defvjp(low_keep, low_pass)
low_back.defvjp(back_keep, back_low)
epsilon = 1e-05
rope_base = 10000.0
highest = lax.Precision.HIGHEST

def product(form, left, right):
    return jnp.einsum(form, left, right, precision=highest)

def layout(lengths, width):
    ends = jnp.cumsum(lengths, -1).astype(jnp.int32)
    places = jnp.arange(width, dtype=jnp.int32)
    segment = lax.optimization_barrier(jnp.sum((places[None, :, None] >= ends[:, None, :]).astype(jnp.int32), -1))
    starts = ends - lengths
    member = segment[:, :, None] == jnp.arange(lengths.shape[-1], dtype=jnp.int32)[None, None, :]
    position = places[None, :] - lax.optimization_barrier(jnp.sum(jnp.where(member, starts[:, None, :], 0), -1))
    allowed = (segment[:, :, None] == segment[:, None, :]) & (places[None, :, None] >= places[None, None, :])
    return (position, allowed)

def turning(position):
    freqs = rope_base ** (-jnp.arange(HEAD_DIM // 2, dtype=jnp.float32) * 2.0 / HEAD_DIM)
    turned = position.astype(jnp.float32)[..., None] * freqs
    return (jnp.cos(turned)[..., None, :], jnp.sin(turned)[..., None, :])

def rotate(values, cosine, sine):
    half = values.shape[-1] // 2
    first = values[..., :half]
    second = values[..., half:]
    return jnp.concatenate([first * cosine - second * sine, second * cosine + first * sine], -1)

def layer(source, params, cosine, sine, allowed, routes):
    gain_one, query_w, key_w, value_w, out_w, gain_two, router_w, gate_w, up_w, down_w = params
    rows, width, model = source.shape
    scale_one = lax.rsqrt(lax.optimization_barrier(jnp.mean(source * source, -1, keepdims=True)) + epsilon)
    normed = low(source * scale_one * gain_one)
    query = low_back(product('rld,de->rle', normed, query_w)).reshape(rows, width, HEADS, HEAD_DIM)
    keys = low_back(product('rld,de->rle', normed, key_w)).reshape(rows, width, KV_HEADS, HEAD_DIM)
    values = low_back(low(product('rld,de->rle', normed, value_w))).reshape(rows, width, KV_HEADS, HEAD_DIM)
    query = low(rotate(query, cosine, sine)).reshape(rows, width, KV_HEADS, HEADS // KV_HEADS, HEAD_DIM)
    keys = low(rotate(keys, cosine, sine))
    scores = low_back(product('rqgjd,rkgd->rgjqk', query, keys) * HEAD_DIM ** (-0.5))
    scores = jnp.where(allowed[:, None, None], scores, -1e+30)
    peak = lax.optimization_barrier(jnp.max(scores, -1, keepdims=True))
    expo = jnp.exp(scores - peak)
    attend = low(expo / lax.optimization_barrier(jnp.sum(expo, -1, keepdims=True)))
    mixed = product('rgjqk,rkgd->rqgjd', attend, values).reshape(rows, width, HEADS * HEAD_DIM)
    mixed = low_back(low(mixed))
    hidden = source + low_back(product('rle,ed->rld', mixed, out_w))
    scale_two = lax.rsqrt(lax.optimization_barrier(jnp.mean(hidden * hidden, -1, keepdims=True)) + epsilon)
    normed_two = low(hidden * scale_two * gain_two)
    logits = low_back(product('rld,de->rle', normed_two, router_w))
    picker = (routes[..., None] == jnp.arange(EXPERTS, dtype=jnp.int32)).astype(jnp.float32)
    picked = lax.optimization_barrier(jnp.sum(logits[:, :, None, :] * picker, -1))
    top_logit = lax.optimization_barrier(jnp.max(picked, -1, keepdims=True))
    raised = jnp.exp(picked - top_logit)
    gates = raised / lax.optimization_barrier(jnp.sum(raised, -1, keepdims=True))
    dense = lax.optimization_barrier(jnp.sum(gates[..., None] * picker, 2))
    gate_act = low_back(product('rld,def->rlef', normed_two, gate_w))
    up_act = low_back(product('rld,def->rlef', normed_two, up_w))
    act = low(gate_act * lax.logistic(gate_act) * up_act)
    expert_out = low_back(low(product('rlef,efd->rled', act, down_w)))
    return hidden + lax.optimization_barrier(jnp.sum(dense[..., None] * expert_out, 2))

def chain(probes, params, block, cosine, sine, allowed, routes):
    current = block
    results = []
    for index in range(N_SECTION):
        layer_params = tuple((item[index] for item in params))
        result = layer(current + probes[index], layer_params, cosine, sine, allowed, routes[index])
        if index + 1 < N_SECTION:
            result = low_back(low(result))
        results.append(result)
        current = result
    return jnp.stack(results)

def reference(inputs, cotangent, lengths, expert_ids, gain_attn, w_query, w_key, w_value, w_out, gain_ffn, w_router, w_gate, w_up, w_down):
    params = tuple((item.astype(jnp.float32) for item in (gain_attn, w_query, w_key, w_value, w_out, gain_ffn, w_router, w_gate, w_up, w_down)))
    width = TOK_DEV
    block_rows = N_FSDP
    blocks = MICRO * N_DP * N_FSDP // block_rows
    source = inputs.astype(jnp.float32).reshape(blocks, block_rows, width, D)
    target = cotangent.astype(jnp.float32).reshape(blocks, block_rows, width, D)
    spans = lengths.reshape(blocks, block_rows, NSEQ)
    routes = jnp.moveaxis(expert_ids.reshape(N_SECTION, blocks, block_rows, width, TOP), 1, 0)

    def visit(totals, item):
        block, back, span, route = item
        position, allowed = layout(span, width)
        cosine, sine = turning(position)
        probes = jnp.zeros((N_SECTION, block_rows, width, D), jnp.float32)

        def run(probes_in, params_in):
            return chain(probes_in, params_in, block, cosine, sine, allowed, route)
        results, pull = jax.vjp(run, probes, params)
        upstream = jnp.concatenate([jnp.zeros((N_SECTION - 1, block_rows, width, D), jnp.float32), back[None]], 0)
        grad_probes, grad_params = pull(upstream)
        totals = tuple((first + second for first, second in zip(totals, grad_params)))
        return (totals, (results.astype(jnp.bfloat16), grad_probes.astype(jnp.bfloat16)))
    start_totals = tuple((jnp.zeros_like(item) for item in params))
    totals, (results, grads) = lax.scan(visit, start_totals, (source, target, spans, routes))
    layer_outputs = jnp.moveaxis(results, 1, 0).reshape(N_SECTION, MICRO, N_DP * N_FSDP * width, D)
    input_grads = jnp.moveaxis(grads, 1, 0).reshape(N_SECTION, MICRO, N_DP * N_FSDP * width, D)
    return (layer_outputs, input_grads, totals[0], totals[1], totals[2], totals[3], totals[4], totals[5], totals[6], totals[7], totals[8], totals[9])
```

```python
import jax
import jax.numpy as jnp
from jax import lax
from jax.sharding import Mesh, PartitionSpec as P

D = 1024
HEAD_DIM = 64
GROUPS = 4
FF = 512
OWN = 4
ROW = 128
epsilon = 1e-05
rope_base = 10000.0
bf16 = jnp.bfloat16
f32 = jnp.float32


def pp(value, axis, step):
    count = lax.axis_size(axis)
    return lax.ppermute(value, axis, [(i, (i + step) % count) for i in range(count)])


def involute(value, dim, index):
    size = value.shape[dim] // 4
    blocks = [lax.slice_in_dim(value, i * size, (i + 1) * size, axis=dim) for i in (3, 2, 1, 0)]
    double = jnp.concatenate(blocks + blocks[:3], dim)
    return lax.dynamic_slice_in_dim(double, (3 - index) * size, 4 * size, dim)


def gather4(value, axis):
    half = value.shape[0] // 2
    left = pp(value, axis, 1)
    right = pp(value, axis, -1)
    far = jnp.concatenate([pp(left[:half], axis, 1), pp(right[half:], axis, -1)], 0)
    return [value, left, far, right]


def plus(first, second):
    return (first.astype(f32) + second.astype(f32)).astype(bf16)


def scatter4(blocks, axis):
    here, behind, far, ahead = blocks
    half = here.shape[0] // 2
    far_up = pp(far[:half], axis, 1)
    far_down = pp(far[half:], axis, -1)
    up_late = pp(ahead[half:], axis, 1)
    down_early = pp(behind[:half], axis, -1)
    up_early = pp(plus(ahead[:half], far_up), axis, 1)
    down_late = pp(plus(behind[half:], far_down), axis, -1)
    first = (here[:half].astype(f32) + up_early.astype(f32) + down_early.astype(f32)).astype(bf16)
    second = (here[half:].astype(f32) + up_late.astype(f32) + down_late.astype(f32)).astype(bf16)
    return jnp.concatenate([first, second], 0)


def other(value):
    return pp(value, "core", 1)


def both(value):
    return jnp.concatenate([value, other(value)], 0)


def flip(value):
    half = value.shape[0] // 2
    return jnp.concatenate([value[half:], value[:half]], 0)


def dot(left, right):
    return jnp.dot(left, right, preferred_element_type=f32)


def dot_t(left, right):
    return lax.dot_general(left, right, (((1,), (1,)), ((), ())), preferred_element_type=f32)


def t_dot(left, right):
    return lax.dot_general(left, right, (((0,), (0,)), ((), ())), preferred_element_type=f32)


def inverse_root(value):
    return lax.rsqrt(jnp.mean(value * value, -1, keepdims=True) + epsilon)


def layout(lengths):
    ends = jnp.cumsum(lengths, -1)
    places = jnp.arange(ROW, dtype=jnp.int32)
    segment = jnp.sum((places[None, :, None] >= ends[:, None, :]).astype(jnp.int32), -1)
    starts = ends - lengths
    member = segment[:, :, None] == jnp.arange(lengths.shape[-1], dtype=jnp.int32)
    position = places[None, :] - jnp.sum(jnp.where(member, starts[:, None, :], 0), -1)
    allowed = (segment[:, :, None] == segment[:, None, :]) & (
        places[None, :, None] >= places[None, None, :]
    )
    freqs = rope_base ** (-jnp.arange(HEAD_DIM // 2, dtype=f32) * 2.0 / HEAD_DIM)
    turned = position.reshape(-1).astype(f32)[:, None] * freqs
    return allowed, jnp.cos(turned)[:, None, :], jnp.sin(turned)[:, None, :]


def rotate(values, cosine, sine):
    shaped = values.reshape(values.shape[0], -1, HEAD_DIM)
    first, second = shaped[..., : HEAD_DIM // 2], shaped[..., HEAD_DIM // 2 :]
    turned = jnp.concatenate([first * cosine - second * sine, second * cosine + first * sine], -1)
    return turned.reshape(values.shape)


def attention_scores(query, keys, allowed):
    rows = query.shape[0] // ROW
    grouped = query.reshape(rows, ROW, GROUPS, 2, HEAD_DIM)
    shaped = keys.reshape(rows, ROW, GROUPS, HEAD_DIM)
    scores = jnp.einsum("rqgjd,rkgd->rgjqk", grouped, shaped, preferred_element_type=f32)
    scores = jnp.where(allowed[:, None, None], scores * HEAD_DIM**-0.5, -1e30)
    expo = jnp.exp(scores - jnp.max(scores, -1, keepdims=True))
    return grouped, shaped, expo / jnp.sum(expo, -1, keepdims=True)


def attention_forward(x, gain, w_qkv, w_out, place):
    allowed, cosine, sine = place
    source = x.astype(f32)
    normed = (source * inverse_root(source) * gain).astype(bf16)
    qkv = dot(normed, w_qkv)
    query = rotate(qkv[:, :512], cosine, sine).astype(bf16)
    keys = rotate(qkv[:, 512:768], cosine, sine).astype(bf16)
    values = qkv[:, 768:].astype(bf16)
    _, _, attend = attention_scores(query, keys, allowed)
    rows = x.shape[0] // ROW
    mixed = jnp.einsum(
        "rgjqk,rkgd->rqgjd",
        attend.astype(bf16),
        values.reshape(rows, ROW, GROUPS, HEAD_DIM),
        preferred_element_type=f32,
    )
    mixed = mixed.reshape(x.shape[0], 512).astype(bf16)
    return normed, query, keys, values, mixed, dot(mixed, w_out).astype(bf16)


def expert_forward(x, part, gain, w_router, w_gate, w_up, w_down, chosen):
    hidden = x.astype(f32) + part[0].astype(f32) + flip(part[1]).astype(f32)
    normed = (hidden * inverse_root(hidden) * gain).astype(bf16)
    logits = dot(normed, w_router)
    masked = jnp.where(chosen > 0, logits, -1e30)
    raised = jnp.where(chosen > 0, jnp.exp(masked - jnp.max(masked, -1, keepdims=True)), 0.0)
    gates = (raised / jnp.sum(raised, -1, keepdims=True))[:, :OWN]
    gate_in = [dot(normed, w_gate[e]) for e in range(OWN)]
    up_in = [dot(normed, w_up[e]) for e in range(OWN)]
    acted = [
        (gates[:, e, None] * gate_in[e] * lax.logistic(gate_in[e]) * up_in[e]).astype(bf16)
        for e in range(OWN)
    ]
    total = sum(dot(acted[e], w_down[e]) for e in range(OWN)).astype(bf16)
    gate_in = [v.astype(bf16) for v in gate_in]
    up_in = [v.astype(bf16) for v in up_in]
    return hidden, normed, gates, gate_in, up_in, acted, total


def expert_backward(grad, moe, record, w_router, w_gate, w_up, w_down, weights):
    hidden, normed, gates, gate_in, up_in, acted = record
    inner = jnp.sum(grad.astype(f32) * moe, -1, keepdims=True)
    total = 0.0
    logit_grads, gate_grads, up_grads = [], [], []
    for e in range(OWN):
        a, b = gate_in[e].astype(f32), up_in[e].astype(f32)
        sigma = lax.logistic(a)
        wide = dot_t(grad, w_down[e])
        slope = jnp.sum(wide * a * sigma * b, -1, keepdims=True)
        logit_grads.append(gates[:, e, None] * (slope - inner))
        wide = wide * gates[:, e, None]
        gate_grads.append((wide * b * sigma * (1.0 + a * (1.0 - sigma))).astype(bf16))
        up_grads.append((wide * a * sigma).astype(bf16))
        total = total + dot_t(gate_grads[e], w_gate[e]) + dot_t(up_grads[e], w_up[e])
    logit_grads = jnp.concatenate(logit_grads, -1).astype(bf16)
    total = (total + dot_t(logit_grads, w_router[:, :OWN])).astype(bf16)
    if not weights:
        return total, None
    grads = (
        t_dot(normed, logit_grads),
        [t_dot(normed, gate_grads[e]).astype(bf16) for e in range(OWN)],
        [t_dot(normed, up_grads[e]).astype(bf16) for e in range(OWN)],
        [t_dot(acted[e], grad).astype(bf16) for e in range(OWN)],
    )
    return total, grads


def norm_backward(grad_normed, value, gain):
    scale = inverse_root(value)
    scaled = grad_normed * gain
    gain_grad = jnp.sum((grad_normed * value * scale)[:256], 0)
    return scale * scaled - value * scale**3 * jnp.mean(value * scaled, -1, keepdims=True), gain_grad


def attention_backward(grad_hidden, record, w_qkv, w_out, place, weights):
    allowed, cosine, sine = place
    normed, query, keys, values, mixed = record
    width = query.shape[0]
    rows = width // ROW
    grad_attn = grad_hidden.astype(bf16)
    grad_mixed = dot_t(grad_attn, w_out).astype(bf16).reshape(rows, ROW, GROUPS, 2, HEAD_DIM)
    grouped, shaped, attend = attention_scores(query, keys, allowed)
    shaped_values = values.reshape(rows, ROW, GROUPS, HEAD_DIM)
    grad_attend = jnp.einsum("rqgjd,rkgd->rgjqk", grad_mixed, shaped_values, preferred_element_type=f32)
    grad_values = jnp.einsum("rgjqk,rqgjd->rkgd", attend.astype(bf16), grad_mixed, preferred_element_type=f32)
    inner = jnp.sum(attend * grad_attend, -1, keepdims=True)
    grad_scores = (attend * (grad_attend - inner) * HEAD_DIM**-0.5).astype(bf16)
    grad_query = jnp.einsum("rgjqk,rkgd->rqgjd", grad_scores, shaped, preferred_element_type=f32)
    grad_keys = jnp.einsum("rgjqk,rqgjd->rkgd", grad_scores, grouped, preferred_element_type=f32)
    grad_query = rotate(grad_query.reshape(width, 512), cosine, -sine)
    grad_keys = rotate(grad_keys.reshape(width, 256), cosine, -sine)
    grad_qkv = jnp.concatenate([grad_query, grad_keys, grad_values.reshape(width, 256)], -1).astype(bf16)
    total = dot_t(grad_qkv, w_qkv).astype(bf16)
    if not weights:
        return total, None
    return total, (t_dot(normed, grad_qkv).astype(bf16), t_dot(mixed, grad_attn).astype(bf16))


def local(
    inputs, cotangent, lengths, expert_ids, gain_attn, w_query, w_key, w_value, w_out,
    gain_ffn, w_router, w_gate, w_up, w_down,
):
    section = lax.axis_index("section")
    x_at, y_at, core = lax.axis_index("x"), lax.axis_index("y"), lax.axis_index("core")

    q_own = lax.dynamic_index_in_dim(w_query[0].reshape(256, 4, 2, 128), core, 2, False).reshape(256, 512)
    k_own = lax.dynamic_index_in_dim(w_key[0].reshape(256, 4, 2, 64), core, 2, False).reshape(256, 256)
    v_own = lax.dynamic_index_in_dim(w_value[0].reshape(256, 4, 2, 64), core, 2, False).reshape(256, 256)
    out_own = lax.dynamic_slice_in_dim(w_out[0], core * 128, 128, 0)
    small = jnp.concatenate([gain_attn[0][None], gain_ffn[0][None], w_router[0].T], 0)
    small = jnp.concatenate([small, jnp.zeros((6, 256), bf16)], 0)
    small_all = jnp.concatenate(gather4(small, "x"), -1)
    qkv_all = jnp.concatenate(gather4(jnp.concatenate([q_own, k_own, v_own], -1), "x"), 0)
    out_all = involute(jnp.concatenate(gather4(out_own, "x"), 0), 0, x_at)
    out_all = involute(out_all, 1, x_at)
    gate_own = involute(
        jnp.swapaxes(lax.dynamic_slice_in_dim(w_gate[0], core * OWN, OWN, 1), 0, 1), 0, y_at
    )
    up_own = involute(
        jnp.swapaxes(lax.dynamic_slice_in_dim(w_up[0], core * OWN, OWN, 1), 0, 1), 0, y_at
    )
    down_own = involute(lax.dynamic_slice_in_dim(w_down[0], core * OWN, OWN, 0), 0, y_at)
    pair = jnp.stack([gate_own[0], up_own[0]], 0)
    pair = jnp.concatenate(gather4(pair, "x"), 1)
    pairs = gather4(pair, "y")
    gate_all = [v[0] for v in pairs]
    up_all = [v[1] for v in pairs]
    down_pieces = gather4(down_own, "x")
    down_all = [jnp.concatenate([v[e] for v in down_pieces], -1) for e in range(OWN)]
    gain_one = small_all[0].astype(f32)
    gain_two = small_all[1].astype(f32)

    marks = jnp.concatenate(
        [expert_ids[0].reshape(256, 4), jnp.broadcast_to(lengths, (2, 128, 4)).reshape(256, 4)], -1
    )
    marks = both(marks)
    ids = marks[:, :4]
    place = layout(marks[:, 4:].reshape(4, 128, 4)[:, 0])
    near = core * OWN + (y_at - jnp.arange(OWN)) % OWN
    slots = jnp.concatenate([near, (near + OWN) % 8])
    chosen = jnp.sum((ids[:, :, None] == slots).astype(jnp.int32), 1)
    router = jnp.take(small_all[2:10].T, slots, axis=1)

    own_x = involute(inputs.reshape(256, D), 1, x_at)
    start = both(own_x)
    x = start
    own_out = None
    for phase in range(2):
        normed, query, keys, values, mixed, part = attention_forward(x, gain_one, qkv_all, out_all, place)
        hidden, normed_two, gates, gate_in, up_in, acted, total = expert_forward(
            x, (part, other(part)), gain_two, router, gate_all, up_all, down_all, chosen
        )
        moe = total.astype(f32) + flip(other(total)).astype(f32)
        own_out = (hidden + moe)[:256].astype(bf16)
        if phase == 0:
            received = lax.ppermute(own_out, "section", [(0, 1)])
            x = jnp.where(section == 0, start, both(received))

    grad = both(involute(cotangent.reshape(256, D), 1, x_at))
    first = grad
    expert_record = (hidden, normed_two, gates, gate_in, up_in, acted)
    attn_record = (normed, query, keys, values, mixed)
    source = x.astype(f32)
    for phase in range(2):
        last = phase == 1
        part, expert_grads = expert_backward(
            grad, moe, expert_record, router, gate_all, up_all, down_all, last
        )
        grad_normed = part.astype(f32) + flip(other(part)).astype(f32)
        change, gain_two_grad = norm_backward(grad_normed, hidden, gain_two)
        grad_hidden = grad.astype(f32) + change
        part, attn_grads = attention_backward(grad_hidden, attn_record, qkv_all, out_all, place, last)
        grad_normed = part.astype(f32) + flip(other(part)).astype(f32)
        change, gain_one_grad = norm_backward(grad_normed, source, gain_one)
        own_grad = (grad_hidden + change)[:256].astype(bf16)
        if not last:
            received = lax.ppermute(own_grad, "section", [(1, 0)])
            grad = jnp.where(section == 1, first, both(received))

    router_grad, gate_grads, up_grads, down_grads = expert_grads
    qkv_grad, out_grad = attn_grads

    pair_blocks = [jnp.stack([gate_grads[e], up_grads[e]], 0) for e in range(OWN)]
    pair_sum = scatter4(pair_blocks, "y")
    pair_sum = scatter4([pair_sum[:, 256 * s : 256 * (s + 1)] for s in range(4)], "x")
    down_blocks = [
        jnp.stack([down_grads[e][:, 256 * s : 256 * (s + 1)] for e in range(OWN)], 0) for s in range(4)
    ]
    down_sum = scatter4(down_blocks, "x")
    down_sum = scatter4([down_sum[e] for e in range(OWN)], "y")
    out_grad = involute(involute(out_grad, 0, x_at), 1, x_at)
    attn_blocks = [
        jnp.concatenate([qkv_grad[256 * s : 256 * (s + 1)], out_grad[128 * s : 128 * (s + 1)]], 0)
        for s in range(4)
    ]
    attn_sum = scatter4(attn_blocks, "x")
    attn_sum = involute(attn_sum, 0, y_at)
    attn_sum = scatter4([attn_sum[96 * s : 96 * (s + 1)] for s in range(4)], "y")

    def finish(value):
        value = plus(value, pp(value, "zh", 1))
        return gather4(value, "y")

    def experts(parts):
        mine = involute(jnp.stack(parts, 0), 0, y_at)
        theirs = other(mine)
        low = jnp.where(core == 0, mine, theirs)
        high = jnp.where(core == 0, theirs, mine)
        return jnp.concatenate([low, high], 0).astype(f32)

    pairs = finish(pair_sum)
    grad_gate = jnp.swapaxes(experts([v[0] for v in pairs]), 0, 1)
    grad_up = jnp.swapaxes(experts([v[1] for v in pairs]), 0, 1)
    grad_down = experts(finish(down_sum))
    attn_own = involute(jnp.concatenate(finish(attn_sum), 0), 0, y_at)
    attn_far = other(attn_own)
    attn_low = jnp.where(core == 0, attn_own, attn_far).astype(f32)
    attn_high = jnp.where(core == 0, attn_far, attn_own).astype(f32)

    def mingle(start_at, size):
        low = attn_low[:256, start_at : start_at + 4 * size].reshape(256, 4, size)
        high = attn_high[:256, start_at : start_at + 4 * size].reshape(256, 4, size)
        return jnp.stack([low, high], 2).reshape(256, 8 * size)

    grad_query = mingle(0, 128)
    grad_key = mingle(512, 64)
    grad_value = mingle(768, 64)
    grad_out = jnp.concatenate([attn_low[256:], attn_high[256:]], 0)

    spread = jnp.zeros((8, D), f32)
    spread = lax.dynamic_update_slice_in_dim(spread, involute(router_grad.T, 0, y_at), core * OWN, 0)
    small_grads = jnp.concatenate(
        [gain_one_grad[None], gain_two_grad[None], spread, jnp.zeros((6, D), f32)], 0
    ).astype(bf16)
    small_sum = scatter4([small_grads[:, 256 * s : 256 * (s + 1)] for s in range(4)], "x")
    small_sum = plus(small_sum, other(small_sum))
    small_sum = plus(small_sum, pp(small_sum, "zh", 1))
    small_sum = sum(v.astype(f32) for v in gather4(small_sum, "y"))

    outputs = involute(own_out, 1, x_at).reshape(2, ROW, D)
    input_grads = involute(own_grad, 1, x_at).reshape(2, ROW, D)
    return (
        outputs[None],
        input_grads[None],
        small_sum[0][None],
        grad_query[None],
        grad_key[None],
        grad_value[None],
        grad_out[None],
        small_sum[1][None],
        small_sum[2:10].T[None],
        grad_gate[None],
        grad_up[None],
        grad_down[None],
    )


def solution(mesh):
    fine = Mesh(mesh.devices.reshape(2, 4, 2, 2, 4), ("section", "y", "zh", "core", "x"))
    rows = ("y", "zh", "core", "x")
    return jax.shard_map(
        local,
        mesh=fine,
        in_specs=(
            P(None, rows, None),
            P(None, rows, None),
            P(None, rows, None),
            P("section", None, rows, None),
            P("section", "x"),
            P("section", "x", None),
            P("section", "x", None),
            P("section", "x", None),
            P("section", "x", None),
            P("section", "x"),
            P("section", "x", None),
            P("section", "x", None, None),
            P("section", "x", None, None),
            P("section", None, None, "x"),
        ),
        out_specs=(
            P("section", None, rows, None),
            P("section", None, rows, None),
            P("section", "x"),
            P("section", "x", None),
            P("section", "x", None),
            P("section", "x", None),
            P("section", "x", None),
            P("section", "x"),
            P("section", "x", None),
            P("section", "x", None, None),
            P("section", "x", None, None),
            P("section", None, None, "x"),
        ),
        check_vma=False,
    )
```

```python
import functools

import jax
import jax.numpy as jnp
from jax import lax
from jax.experimental import pallas as pl
from jax.experimental.pallas import tpu as pltpu
from jax.sharding import Mesh, PartitionSpec as P

D = 1024
HEAD_DIM = 64
GROUPS = 4
FF = 512
OWN = 4
ROW = 128
epsilon = 1e-05
rope_base = 10000.0
bf16 = jnp.bfloat16
f32 = jnp.float32


def pp(value, axis, step):
    count = lax.axis_size(axis)
    return lax.ppermute(value, axis, [(i, (i + step) % count) for i in range(count)])


def involute(value, dim, index):
    size = value.shape[dim] // 4
    blocks = [lax.slice_in_dim(value, i * size, (i + 1) * size, axis=dim) for i in (3, 2, 1, 0)]
    double = jnp.concatenate(blocks + blocks[:3], dim)
    return lax.dynamic_slice_in_dim(double, (3 - index) * size, 4 * size, dim)


def plus(first, second):
    return (first.astype(f32) + second.astype(f32)).astype(bf16)


def ring3(value, axis):
    return [value, pp(value, axis, 1), pp(value, axis, 2), pp(value, axis, -1)]


def scatter3(blocks, axis):
    here, behind, far, ahead = blocks
    total = here.astype(f32) + pp(ahead, axis, 1).astype(f32)
    total = total + pp(behind, axis, -1).astype(f32) + pp(far, axis, 2).astype(f32)
    return total.astype(bf16)


def other(value):
    return pp(value, "core", 1)


def both(value):
    return jnp.concatenate([value, other(value)], 0)


def flip(value):
    half = value.shape[0] // 2
    return jnp.concatenate([value[half:], value[:half]], 0)


def dot(left, right):
    return jnp.dot(left, right, preferred_element_type=f32)


def dot_t(left, right):
    return lax.dot_general(left, right, (((1,), (1,)), ((), ())), preferred_element_type=f32)


def t_dot(left, right):
    return lax.dot_general(left, right, (((0,), (0,)), ((), ())), preferred_element_type=f32)


def inverse_root(value):
    return lax.rsqrt(jnp.mean(value * value, -1, keepdims=True) + epsilon)


def layout(lengths):
    ends = jnp.cumsum(lengths, -1)
    places = jnp.arange(ROW, dtype=jnp.int32)
    segment = jnp.sum((places[None, :, None] >= ends[:, None, :]).astype(jnp.int32), -1)
    starts = ends - lengths
    member = segment[:, :, None] == jnp.arange(lengths.shape[-1], dtype=jnp.int32)
    position = places[None, :] - jnp.sum(jnp.where(member, starts[:, None, :], 0), -1)
    allowed = (segment[:, :, None] == segment[:, None, :]) & (
        places[None, :, None] >= places[None, None, :]
    )
    freqs = rope_base ** (-jnp.arange(HEAD_DIM // 2, dtype=f32) * 2.0 / HEAD_DIM)
    turned = position.reshape(-1).astype(f32)[:, None] * jnp.tile(freqs, 4)
    sign = jnp.where(jnp.arange(ROW) % HEAD_DIM < HEAD_DIM // 2, -1.0, 1.0).astype(f32)
    return jnp.where(allowed, 0.0, -1e30).astype(f32), jnp.cos(turned), jnp.sin(turned) * sign


def lanes(rows):
    return lax.broadcasted_iota(jnp.int32, (rows, ROW), 1)


def turn(value, cosine, sine):
    lane = lanes(value.shape[0])
    swapped = jnp.where(lane % HEAD_DIM < HEAD_DIM // 2, pltpu.roll(value, 96, 1), pltpu.roll(value, 32, 1))
    return value * cosine + swapped * sine


def doubled(value):
    low = lanes(value.shape[0]) < HEAD_DIM
    rolled = pltpu.roll(value, HEAD_DIM, 1)
    return jnp.where(low, value, rolled), jnp.where(low, rolled, value)


def split_heads(value):
    low = (lanes(1) < HEAD_DIM).astype(f32).astype(bf16)
    return jnp.concatenate([value * low, value * (1 - low)], 0)


def join_heads(value):
    half = value.shape[0] // 2
    return jnp.where(lanes(half) < HEAD_DIM, value[:half], value[half:])


def attend(query, keys, bias):
    scores = dot_t(query, keys) * HEAD_DIM**-0.5 + bias
    expo = jnp.exp(scores - jnp.max(scores, -1, keepdims=True))
    return expo / jnp.sum(expo, -1, keepdims=True)


def attention_forward_kernel(
    x_ref, gain_ref, *refs
):
    cos_ref, sin_ref, bias_ref, n_ref, q_ref, k_ref, v_ref, o_ref, part_ref, w_qkv, w_out, sems = refs[4:]
    bring_attention(refs[:4], w_qkv, w_out, sems)
    source = x_ref[...].astype(f32)
    n_ref[...] = (source * inverse_root(source) * gain_ref[...]).astype(bf16)
    cosine, sine = cos_ref[...], sin_ref[...]
    for c in range(4):
        wide = dot(n_ref[...], w_qkv[:, 256 * c : 256 * (c + 1)])
        for h in range(2):
            value = wide[:, ROW * h : ROW * (h + 1)]
            if c < 2:
                at = ROW * (2 * c + h)
                q_ref[:, at : at + ROW] = turn(value, cosine, sine).astype(bf16)
                continue
            to = k_ref
            if c == 2:
                value = turn(value, cosine, sine)
            else:
                to = v_ref
            first, second = doubled(value)
            to[:, 256 * h : 256 * h + ROW] = first.astype(bf16)
            to[:, 256 * h + ROW : 256 * (h + 1)] = second.astype(bf16)
    for r in range(2):
        rows = slice(ROW * r, ROW * (r + 1))
        bias = jnp.concatenate([bias_ref[r], bias_ref[r]], 0)
        for g in range(GROUPS):
            cols = slice(ROW * g, ROW * (g + 1))
            prob = attend(split_heads(q_ref[rows, cols]), k_ref[rows, cols], bias).astype(bf16)
            o_ref[rows, cols] = join_heads(dot(prob, v_ref[rows, cols])).astype(bf16)
    part_ref[...] = dot(o_ref[...], w_out[...]).astype(bf16)


def spec(shape, index):
    return pl.BlockSpec(shape, index)


def fixed(shape):
    return pl.BlockSpec(shape, lambda i: (0,) * len(shape))


def shape_of(shape, dtype):
    return jax.ShapeDtypeStruct(shape, dtype)


def params():
    return pltpu.CompilerParams(vmem_limit_bytes=56 * 2**20)


def rows_spec(width):
    return pl.BlockSpec((256, width), lambda i: (i, 0))


def ring_place(s):
    return lax.rem(lax.axis_index("x") - s + 4, 4)


def bring_attention(pieces, w_qkv, w_out, sems):
    @pl.when(pl.program_id(0) == 0)
    def _():
        copies = []
        for s in range(4):
            at = ring_place(s)
            to = w_qkv.at[pl.ds(pl.multiple_of(at * 256, 256), 256)]
            copies.append(pltpu.make_async_copy(pieces[s].at[pl.ds(0, 256)], to, sems.at[2 * s]))
            to = w_out.at[pl.ds(pl.multiple_of(at * ROW, ROW), ROW)]
            copies.append(pltpu.make_async_copy(pieces[s].at[pl.ds(256, ROW)], to, sems.at[2 * s + 1]))
        for copy in copies:
            copy.start()
        for copy in copies:
            copy.wait()


def attention_buffers():
    return [pltpu.VMEM((D, D), bf16), pltpu.VMEM((512, D), bf16), pltpu.SemaphoreType.DMA((8,))]


def attention_forward(x, gain, w_attn, place):
    bias, cosine, sine = place
    return pl.pallas_call(
        attention_forward_kernel,
        grid=(2,),
        in_specs=[
            rows_spec(D), fixed((1, D)), *[afar()] * 4, rows_spec(ROW), rows_spec(ROW),
            spec((2, ROW, ROW), lambda i: (i, 0, 0)),
        ],
        out_specs=[rows_spec(w) for w in (D, 512, 512, 512, 512, D)],
        out_shape=[shape_of((512, w), bf16) for w in (D, 512, 512, 512, 512, D)],
        scratch_shapes=attention_buffers(),
        compiler_params=params(),
        cost_estimate=pl.CostEstimate(flops=6 * 10**9, bytes_accessed=10 * 2**20, transcendentals=10**6),
        name="attention_forward",
    )(x, gain, *w_attn, cosine, sine, bias)


def weight_copies(weights, buffers, sems):
    own, left, far_gate, far_up, right, down, down_left, down_far, down_far_too, down_right = weights
    gate, up, low = buffers
    sources = [(own.at[0], own.at[1]), (left.at[0], left.at[1]), (far_gate.at[0], far_up.at[0]), (right.at[0], right.at[1])]
    copies = []
    for e in range(OWN):
        low_from = [down.at[e], down_left.at[e], (down_far, down_far_too)[e // 2].at[e % 2], down_right.at[e]]
        group = []
        for s in range(4):
            at = pl.ds(pl.multiple_of(ring_place(s) * 256, 256), 256)
            group.append((sources[e][0].at[s], gate.at[e, at]))
            group.append((sources[e][1].at[s], up.at[e, at]))
            group.append((low_from[s], low.at[e, :, at]))
        copies.append([pltpu.make_async_copy(*pair, sems.at[12 * e + i]) for i, pair in enumerate(group)])
    return copies


def weight_buffers():
    return [
        pltpu.VMEM((OWN, D, FF), bf16),
        pltpu.VMEM((OWN, D, FF), bf16),
        pltpu.VMEM((OWN, FF, D), bf16),
        pltpu.SemaphoreType.DMA((12 * OWN,)),
    ]


def expert_forward_kernel(save, *refs):
    x_ref, part_ref, far_ref, gain_ref, router_ref, chosen_ref = refs[:6]
    weights, refs = refs[6:16], refs[16:]
    if save:
        h_ref, total_ref, n_ref, gates_ref, *stores = refs[:7]
        refs = refs[7:]
    else:
        h_ref, total_ref = refs[:2]
        n_ref, gates_ref = refs[-2:]
        refs = refs[2:-2]
    gate_ref, up_ref, down_ref, sems, acc_ref = refs[:5]
    if save:
        held, out_sems = refs[5:8], refs[8]
    copies = weight_copies(weights, (gate_ref, up_ref, down_ref), sems)
    for group in copies:
        for copy in group:
            copy.start()
    for i in range(4):
        rows = slice(ROW * i, ROW * (i + 1))
        away = slice(ROW * ((i + 2) % 4), ROW * ((i + 2) % 4 + 1))
        hidden = x_ref[rows].astype(f32) + part_ref[rows].astype(f32) + far_ref[away].astype(f32)
        h_ref[rows] = hidden
        normed = (hidden * inverse_root(hidden) * gain_ref[...]).astype(bf16)
        n_ref[rows] = normed
        on = chosen_ref[rows] > 0
        masked = jnp.where(on, dot(normed, router_ref[...]), -1e30)
        raised = jnp.where(on, jnp.exp(masked - jnp.max(masked, -1, keepdims=True)), 0.0)
        gates_ref[rows] = raised / jnp.sum(raised, -1, keepdims=True)
    sent = []
    for e in range(OWN):
        for copy in copies[e]:
            copy.wait()
        cols = slice(FF * e, FF * (e + 1))
        for i in range(2):
            rows = slice(256 * i, 256 * (i + 1))
            gate = jnp.sum(jnp.where(lanes(256) == e, gates_ref[rows], 0.0), -1, keepdims=True)
            a = dot(n_ref[rows], gate_ref[e])
            b = dot(n_ref[rows], up_ref[e])
            acted = (gate * a * lax.logistic(a) * b).astype(bf16)
            if save:
                held[0][rows, cols] = a.astype(bf16)
                held[1][rows, cols] = b.astype(bf16)
                held[2][rows, cols] = acted
            added = dot(acted, down_ref[e])
            if e == 0:
                acc_ref[rows] = added
            elif e < OWN - 1:
                acc_ref[rows] += added
            else:
                total_ref[rows] = (acc_ref[rows] + added).astype(bf16)
        if save:
            for i in range(3):
                copy = pltpu.make_async_copy(held[i].at[:, cols], stores[i].at[:, cols], out_sems.at[3 * e + i])
                copy.start()
                sent.append(copy)
    for copy in sent:
        copy.wait()


def whole():
    return pl.BlockSpec(memory_space=pltpu.VMEM)


def afar():
    return pl.BlockSpec(memory_space=pl.ANY)


def expert_forward(x, part, far, gain, router, chosen, weights, save):
    out_specs = [whole()] * 2
    out_shape = [shape_of((512, D), f32), shape_of((512, D), bf16)]
    scratch = weight_buffers() + [pltpu.VMEM((512, D), f32)]
    if save:
        out_specs += [whole()] * 2 + [afar()] * 3
        out_shape += [shape_of((512, D), bf16), shape_of((512, ROW), f32)] + [shape_of((512, 2048), bf16)] * 3
        scratch += [pltpu.VMEM((512, 2048), bf16)] * 3 + [pltpu.SemaphoreType.DMA((3 * OWN,))]
    else:
        scratch += [pltpu.VMEM((512, D), bf16), pltpu.VMEM((512, ROW), f32)]
    return pl.pallas_call(
        functools.partial(expert_forward_kernel, save),
        in_specs=[whole()] * 6 + [afar()] * 10,
        out_specs=out_specs,
        out_shape=out_shape,
        scratch_shapes=scratch,
        compiler_params=params(),
        cost_estimate=pl.CostEstimate(flops=7 * 10**9, bytes_accessed=24 * 2**20, transcendentals=10**6),
        name="expert_forward",
    )(x, part, far, gain, router, chosen, *weights)


def expert_backward_kernel(*refs):
    grad_ref, total_ref, far_ref, gates_ref, router_ref, a_ref, b_ref = refs[:7]
    weights = refs[7:17]
    logit_ref, part_ref, *stores = refs[17:21]
    gate_ref, up_ref, down_ref, sems, acc_ref, slope_ref, a_in, b_in, a_out, b_out, row_sems = refs[21:]
    copies = weight_copies(weights, (gate_ref, up_ref, down_ref), sems)
    for e in range(OWN):
        cols = slice(FF * e, FF * (e + 1))
        copies[e].append(pltpu.make_async_copy(a_ref.at[:, cols], a_in.at[:, cols], row_sems.at[4 * e]))
        copies[e].append(pltpu.make_async_copy(b_ref.at[:, cols], b_in.at[:, cols], row_sems.at[4 * e + 1]))
        for copy in copies[e]:
            copy.start()
    inner = []
    for i in range(4):
        rows = slice(ROW * i, ROW * (i + 1))
        away = slice(ROW * ((i + 2) % 4), ROW * ((i + 2) % 4 + 1))
        moe = total_ref[rows].astype(f32) + far_ref[away].astype(f32)
        inner.append(jnp.sum(grad_ref[rows].astype(f32) * moe, -1, keepdims=True))
    inner = [jnp.concatenate(inner[2 * i : 2 * i + 2], 0) for i in range(2)]
    sent = []
    for e in range(OWN):
        for copy in copies[e]:
            copy.wait()
        cols = slice(FF * e, FF * (e + 1))
        for i in range(2):
            rows = slice(256 * i, 256 * (i + 1))
            mine = lanes(256) == e
            gate = jnp.sum(jnp.where(mine, gates_ref[rows], 0.0), -1, keepdims=True)
            wide = dot_t(grad_ref[rows], down_ref[e])
            a, b = a_in[rows, cols].astype(f32), b_in[rows, cols].astype(f32)
            sigma = lax.logistic(a)
            raised = wide * a * sigma
            slope = jnp.where(mine, gate * (jnp.sum(raised * b, -1, keepdims=True) - inner[i]), 0.0)
            a_out[rows, cols] = (gate * wide * b * sigma * (1.0 + a * (1.0 - sigma))).astype(bf16)
            b_out[rows, cols] = (gate * raised).astype(bf16)
            added = dot_t(a_out[rows, cols], gate_ref[e]) + dot_t(b_out[rows, cols], up_ref[e])
            if e == 0:
                slope_ref[rows] = slope
                acc_ref[rows] = added
            elif e < OWN - 1:
                slope_ref[rows] += slope
                acc_ref[rows] += added
            else:
                logit_ref[rows] = (slope_ref[rows] + slope).astype(bf16)
                added = added + dot_t(logit_ref[rows], router_ref[...])
                part_ref[rows] = (acc_ref[rows] + added).astype(bf16)
        for i, held in enumerate((a_out, b_out)):
            copy = pltpu.make_async_copy(held.at[:, cols], stores[i].at[:, cols], row_sems.at[4 * e + 2 + i])
            copy.start()
            sent.append(copy)
    for copy in sent:
        copy.wait()


def expert_backward(grad, total, far, gates, router, a, b, weights):
    return pl.pallas_call(
        expert_backward_kernel,
        in_specs=[whole()] * 5 + [afar()] * 12,
        out_specs=[whole()] * 2 + [afar()] * 2,
        out_shape=[shape_of((512, ROW), bf16), shape_of((512, D), bf16)] + [shape_of((512, 2048), bf16)] * 2,
        scratch_shapes=weight_buffers()
        + [pltpu.VMEM((512, D), f32), pltpu.VMEM((512, ROW), f32)]
        + [pltpu.VMEM((512, 2048), bf16)] * 4
        + [pltpu.SemaphoreType.DMA((4 * OWN,))],
        compiler_params=params(),
        cost_estimate=pl.CostEstimate(flops=7 * 10**9, bytes_accessed=24 * 2**20, transcendentals=10**6),
        name="expert_backward",
    )(grad, total, far, gates, router, a, b, *weights)


def spread_kernel(pair, pair_far, low, low_far, attn, attn_far, mix, mix_far, gate, up, down, query, key, value, out):
    first = lax.axis_index("core") == 0

    def sides(near, far):
        near, far = near.astype(f32), far.astype(f32)
        return jnp.where(first, near, far), jnp.where(first, far, near)

    for y in range(4):
        for c, side in enumerate(sides(pair[y], pair_far[y])):
            gate[:, 4 * c + y, :] = side[:, :FF]
            up[:, 4 * c + y, :] = side[:, FF:]
        for c, side in enumerate(sides(low[y], low_far[y])):
            down[4 * c + y] = side
    for c, side in enumerate(sides(mix[0], mix_far[0])):
        out[c] = side
    near, far = sides(attn[0], attn_far[0])
    below = lanes(64) < HEAD_DIM
    for s in range(4):
        query[:, 256 * s : 256 * s + ROW] = near[:, ROW * s : ROW * (s + 1)]
        query[:, 256 * s + ROW : 256 * (s + 1)] = far[:, ROW * s : ROW * (s + 1)]
    for to, base in ((key, 512), (value, 768)):
        for h in range(2):
            a = near[:, base + ROW * h : base + ROW * (h + 1)]
            b = far[:, base + ROW * h : base + ROW * (h + 1)]
            to[:, 256 * h : 256 * h + ROW] = jnp.where(below, a, pltpu.roll(b, HEAD_DIM, 1))
            to[:, 256 * h + ROW : 256 * (h + 1)] = jnp.where(below, pltpu.roll(a, HEAD_DIM, 1), b)


def spread(packed, theirs):
    specs = [
        spec((4, 64, D), lambda i: (0, i, 0)),
        spec((4, ROW, 256), lambda i: (0, 2, i)),
        spec((1, 64, D), lambda i: (i, 6, 0)),
        spec((1, 32, D), lambda i: (i, 14, 0)),
    ]
    return pl.pallas_call(
        spread_kernel,
        grid=(4,),
        in_specs=[item for item in specs for _ in range(2)],
        out_specs=[
            spec((64, 8, FF), lambda i: (i, 0, 0)),
            spec((64, 8, FF), lambda i: (i, 0, 0)),
            spec((8, ROW, 256), lambda i: (0, i, 0)),
            spec((64, D), lambda i: (i, 0)),
            spec((64, 512), lambda i: (i, 0)),
            spec((64, 512), lambda i: (i, 0)),
            spec((2, 32, D), lambda i: (0, i, 0)),
        ],
        out_shape=[
            shape_of(shape, f32)
            for shape in ((256, 8, FF), (256, 8, FF), (8, FF, 256), (256, D), (256, 512), (256, 512), (2, ROW, D))
        ],
        compiler_params=params(),
        cost_estimate=pl.CostEstimate(flops=10**6, bytes_accessed=24 * 2**20, transcendentals=0),
        name="spread",
    )(*[packed, theirs] * 4)


def norm_backward(grad_normed, value, gain):
    scale = inverse_root(value)
    scaled = grad_normed * gain
    change = scale * scaled - value * scale**3 * jnp.mean(value * scaled, -1, keepdims=True)
    return change, jnp.sum(grad_normed * value * scale, 0, keepdims=True)


def attention_backward_kernel(
    grad_ref, h_ref, near_ref, far_ref, gain_ref, *refs
):
    q_ref, k_ref, v_ref, cos_ref, sin_ref, bias_ref = refs[4:10]
    dh_ref, da_ref, dqkv_ref, part_ref, gain_grad_ref, do_ref, w_qkv, w_out, sems = refs[10:]
    bring_attention(refs[:4], w_qkv, w_out, sems)
    change, gain_grad = norm_backward(
        near_ref[...].astype(f32) + far_ref[...].astype(f32), h_ref[...], gain_ref[...]
    )

    @pl.when(pl.program_id(0) == 0)
    def _():
        gain_grad_ref[...] = gain_grad

    grad_hidden = grad_ref[...].astype(f32) + change
    dh_ref[...] = grad_hidden
    da_ref[...] = grad_hidden.astype(bf16)
    do_ref[...] = dot_t(da_ref[...], w_out[...]).astype(bf16)
    for r in range(2):
        rows = slice(ROW * r, ROW * (r + 1))
        bias = jnp.concatenate([bias_ref[r], bias_ref[r]], 0)
        cosine, sine = cos_ref[rows], -sin_ref[rows]
        key_grads, value_grads = [], []
        for g in range(GROUPS):
            cols = slice(ROW * g, ROW * (g + 1))
            query = split_heads(q_ref[rows, cols])
            keys = k_ref[rows, cols]
            prob = attend(query, keys, bias)
            grad_mixed = split_heads(do_ref[rows, cols])
            grad_prob = dot_t(grad_mixed, v_ref[rows, cols])
            value_grads.append(t_dot(prob.astype(bf16), grad_mixed))
            inner = jnp.sum(prob * grad_prob, -1, keepdims=True)
            grad_scores = (prob * (grad_prob - inner) * HEAD_DIM**-0.5).astype(bf16)
            dqkv_ref[rows, cols] = turn(join_heads(dot(grad_scores, keys)), cosine, sine).astype(bf16)
            key_grads.append(t_dot(grad_scores, query))
        for h in range(2):
            low = lanes(ROW) < HEAD_DIM
            pair = [v + pltpu.roll(v, HEAD_DIM, 1) for v in key_grads[2 * h : 2 * h + 2]]
            at = 512 + ROW * h
            dqkv_ref[rows, at : at + ROW] = turn(jnp.where(low, *pair), cosine, sine).astype(bf16)
            pair = [v + pltpu.roll(v, HEAD_DIM, 1) for v in value_grads[2 * h : 2 * h + 2]]
            at = 768 + ROW * h
            dqkv_ref[rows, at : at + ROW] = jnp.where(low, *pair).astype(bf16)
    part_ref[...] = dot_t(dqkv_ref[...], w_qkv[...]).astype(bf16)


def attention_backward(grad, hidden, near, far, gain, w_attn, query, keys, values, place):
    bias, cosine, sine = place
    return pl.pallas_call(
        attention_backward_kernel,
        grid=(2,),
        in_specs=[
            rows_spec(D), rows_spec(D), rows_spec(D), pl.BlockSpec((256, D), lambda i: (1 - i, 0)),
            fixed((1, D)), *[afar()] * 4,
            rows_spec(512), rows_spec(512), rows_spec(512), rows_spec(ROW), rows_spec(ROW),
            spec((2, ROW, ROW), lambda i: (i, 0, 0)),
        ],
        out_specs=[rows_spec(D)] * 4 + [fixed((1, D))],
        out_shape=[shape_of((512, D), f32)] + [shape_of((512, D), bf16)] * 3 + [shape_of((1, D), f32)],
        scratch_shapes=[pltpu.VMEM((256, 512), bf16)] + attention_buffers(),
        compiler_params=params(),
        cost_estimate=pl.CostEstimate(flops=9 * 10**9, bytes_accessed=16 * 2**20, transcendentals=10**6),
        name="attention_backward",
    )(grad, hidden, near, far, gain, *w_attn, query, keys, values, cosine, sine, bias)


def local(
    inputs, cotangent, lengths, expert_ids, gain_attn, w_query, w_key, w_value, w_out,
    gain_ffn, w_router, w_gate, w_up, w_down,
):
    section = lax.axis_index("section")
    x_at, y_at, core = lax.axis_index("x"), lax.axis_index("y"), lax.axis_index("core")

    expert = core * OWN + y_at
    pair = jnp.stack(
        [lax.dynamic_index_in_dim(w_gate[0], expert, 1, False), lax.dynamic_index_in_dim(w_up[0], expert, 1, False)], 0
    )
    pair = jnp.stack(ring3(pair, "x"), 1)
    q_own = lax.dynamic_index_in_dim(w_query[0].reshape(256, 4, 2, 128), core, 2, False).reshape(256, 512)
    k_own = lax.dynamic_index_in_dim(w_key[0].reshape(256, 4, 2, 64), core, 2, False).reshape(256, 256)
    v_own = lax.dynamic_index_in_dim(w_value[0].reshape(256, 4, 2, 64), core, 2, False).reshape(256, 256)
    out_own = lax.dynamic_slice_in_dim(w_out[0], core * 128, 128, 0)
    small = jnp.concatenate([gain_attn[0], gain_ffn[0], w_router[0].T.reshape(2048)])
    small = jnp.concatenate([small, jnp.zeros((16 * D - 2560,), bf16)]).reshape(16, D)
    attn_own = jnp.concatenate([jnp.concatenate([q_own, k_own, v_own], -1), out_own, small], 0)
    down_own = involute(lax.dynamic_slice_in_dim(w_down[0], core * OWN, OWN, 0), 0, y_at)
    attn_own, down_own, pair = lax.optimization_barrier((attn_own, down_own, pair))
    left, right = pp(pair, "y", 1), pp(pair, "y", -1)
    attn_all = ring3(attn_own, "x")
    down_left, down_right = pp(down_own, "x", 1), pp(down_own, "x", -1)
    far_gate, far_up = pp(left[:1], "y", 1), pp(right[1:], "y", -1)
    down_far, down_far_too = pp(down_left[:2], "x", 1), pp(down_right[2:], "x", -1)
    weights = (pair, left, far_gate, far_up, right, down_own, down_left, down_far, down_far_too, down_right)
    small_all = jnp.concatenate([v[384:387].reshape(12, 256) for v in attn_all], -1)
    small_all = involute(small_all, 1, x_at)
    gain_one = small_all[:1].astype(f32)
    gain_two = small_all[1:2].astype(f32)

    marks = jnp.concatenate(
        [expert_ids[0].reshape(256, 4), jnp.broadcast_to(lengths, (2, 128, 4)).reshape(256, 4)], -1
    )
    marks = both(marks)
    ids = marks[:, :4]
    place = layout(marks[:, 4:].reshape(4, 128, 4)[:, 0])
    near = core * OWN + (y_at - jnp.arange(OWN)) % OWN
    slots = jnp.concatenate([near, (near + OWN) % 8, jnp.full((ROW - 8,), -1)])
    chosen = jnp.sum((ids[:, :, None] == slots).astype(f32), 1)
    router = t_dot(small_all[2:10], (jnp.arange(8)[:, None] == slots).astype(bf16)).astype(bf16)

    start = both(inputs.reshape(256, D))
    x = start
    for phase in range(2):
        normed, query, keys, values, mixed, part = attention_forward(x, gain_one, attn_all, place)
        hidden, total, *record = expert_forward(
            x, part, other(part), gain_two, router, chosen, weights, phase == 1
        )
        total_far = other(total)
        moe = total[:256].astype(f32) + total_far[256:].astype(f32)
        own_out = (hidden[:256] + moe).astype(bf16)
        if phase == 0:
            received = lax.ppermute(own_out, "section", [(0, 1)])
            x = jnp.where(section == 0, start, both(received))

    normed_two, gates, gate_in, up_in, acted = record
    grad = both(cotangent.reshape(256, D))
    first = grad
    source = x[:256].astype(f32)
    for phase in range(2):
        logit_grad, part, gate_grad, up_grad = expert_backward(
            grad, total, total_far, gates, router, gate_in, up_in, weights
        )
        if phase == 1:
            down_grad = t_dot(acted, grad).astype(bf16).reshape(OWN, FF, D)
            gate_grad = t_dot(normed_two, gate_grad).astype(bf16)
            up_grad = t_dot(normed_two, up_grad).astype(bf16)
            part, gate_grad, up_grad, down_grad = lax.optimization_barrier(
                (part, gate_grad, up_grad, down_grad)
            )
            blocks = [
                jnp.concatenate([gate_grad[:, FF * e : FF * (e + 1)], up_grad[:, FF * e : FF * (e + 1)]], -1)
                for e in range(OWN)
            ]
            far_sent = (pp(blocks[2][:512], "y", 1), pp(blocks[2][512:], "y", -1))
            down_sum = lax.psum_scatter(down_grad, "x", scatter_dimension=2, tiled=True)
        grad_hidden, grad_attn, qkv_grad, part, gain_two_grad = attention_backward(
            grad, hidden, part, other(part), gain_two, attn_all, query, keys, values, place
        )
        if phase == 1:
            far_sent, part = lax.optimization_barrier((far_sent, part))
            ahead = jnp.concatenate([plus(blocks[3][:512], far_sent[0]), blocks[3][512:]], 0)
            behind = jnp.concatenate([blocks[1][:512], plus(blocks[1][512:], far_sent[1])], 0)
            ahead, behind = pp(ahead, "y", 1), pp(behind, "y", -1)
        far = other(part)
        grad_normed = part[:256].astype(f32) + far[256:].astype(f32)
        change, gain_one_grad = norm_backward(grad_normed, source, gain_one)
        own_grad = (grad_hidden[:256] + change).astype(bf16)
        if phase == 0:
            received = lax.ppermute(own_grad, "section", [(1, 0)])
            grad = jnp.where(section == 1, first, both(received))

    router_grad = t_dot(normed_two, logit_grad)[:, :OWN]
    qkv_grad = t_dot(normed, qkv_grad).astype(bf16)
    out_grad = t_dot(mixed, grad_attn).astype(bf16)
    placed = jnp.zeros((8, D), f32)
    placed = lax.dynamic_update_slice_in_dim(placed, involute(router_grad.T, 0, y_at), core * OWN, 0)
    small_grads = jnp.concatenate([gain_one_grad, gain_two_grad, placed], 0).astype(bf16)

    def block(s):
        small = small_grads[:, 256 * s : 256 * (s + 1)].reshape(2560)
        small = jnp.concatenate([small, jnp.zeros((32 * D - 2560,), bf16)]).reshape(32, D)
        return jnp.concatenate(
            [qkv_grad[256 * s : 256 * (s + 1)], out_grad[128 * s : 128 * (s + 1)], small], 0
        )

    attn_sum = lax.psum_scatter(jnp.stack([block(s) for s in range(4)], 0), "x", scatter_dimension=0)
    pair_sum = (blocks[0].astype(f32) + ahead.astype(f32) + behind.astype(f32)).astype(bf16)
    pair_sum = involute(pair_sum, 0, x_at)
    pair_sum = scatter3([pair_sum[256 * s : 256 * (s + 1)] for s in range(4)], "x")
    parts = [(attn_sum[:256], 64), (attn_sum[256:384], 32), (attn_sum[384:], 8)]
    parts = [(involute(part, 0, y_at), size) for part, size in parts]

    def rest(e):
        down = jnp.concatenate([down_sum[e, ROW * i : ROW * (i + 1)] for i in range(4)], -1)
        return jnp.concatenate([down] + [part[size * e : size * (e + 1)] for part, size in parts], 0)

    rest_sum = scatter3([rest(e) for e in range(OWN)], "y")

    packed = jnp.concatenate([pair_sum, rest_sum], 0)
    packed = plus(packed, pp(packed, "zh", 1))
    packed = lax.all_gather(packed, "y")
    theirs = other(packed)
    grad_gate, grad_up, grad_down, grad_query, grad_key, grad_value, grad_out = spread(packed, theirs)
    grad_out = grad_out.reshape(256, D)
    small_sum = (packed[0, 480:483].astype(f32) + theirs[0, 480:483].astype(f32)).reshape(12, 256)

    outputs = own_out.reshape(2, ROW, D)
    input_grads = own_grad.reshape(2, ROW, D)
    return (
        outputs[None],
        input_grads[None],
        small_sum[0][None],
        grad_query[None],
        grad_key[None],
        grad_value[None],
        grad_out[None],
        small_sum[1][None],
        small_sum[2:10].T[None],
        grad_gate[None],
        grad_up[None],
        grad_down[None],
    )


def solution(mesh):
    fine = Mesh(mesh.devices.reshape(2, 4, 2, 2, 4), ("section", "y", "zh", "core", "x"))
    rows = ("y", "zh", "core", "x")
    return jax.shard_map(
        local,
        mesh=fine,
        in_specs=(
            P(None, rows, None),
            P(None, rows, None),
            P(None, rows, None),
            P("section", None, rows, None),
            P("section", "x"),
            P("section", "x", None),
            P("section", "x", None),
            P("section", "x", None),
            P("section", "x", None),
            P("section", "x"),
            P("section", "x", None),
            P("section", "x", None, None),
            P("section", "x", None, None),
            P("section", None, None, "x"),
        ),
        out_specs=(
            P("section", None, rows, None),
            P("section", None, rows, None),
            P("section", "x"),
            P("section", "x", None),
            P("section", "x", None),
            P("section", "x", None),
            P("section", "x", None),
            P("section", "x"),
            P("section", "x", None),
            P("section", "x", None, None),
            P("section", "x", None, None),
            P("section", None, None, "x"),
        ),
        check_vma=False,
    )
```

```python
import functools

import jax
import jax.numpy as jnp
from jax import lax
from jax.experimental import pallas as pl
from jax.experimental.pallas import tpu as pltpu
from jax.sharding import Mesh, PartitionSpec as P

D = 1024
HEAD_DIM = 64
GROUPS = 4
FF = 512
OWN = 4
ROW = 128
epsilon = 1e-05
rope_base = 10000.0
bf16 = jnp.bfloat16
f32 = jnp.float32


def pp(value, axis, step):
    count = lax.axis_size(axis)
    return lax.ppermute(value, axis, [(i, (i + step) % count) for i in range(count)])


def involute(value, dim, index):
    size = value.shape[dim] // 4
    blocks = [lax.slice_in_dim(value, i * size, (i + 1) * size, axis=dim) for i in (3, 2, 1, 0)]
    double = jnp.concatenate(blocks + blocks[:3], dim)
    return lax.dynamic_slice_in_dim(double, (3 - index) * size, 4 * size, dim)


def plus(first, second):
    return (first.astype(f32) + second.astype(f32)).astype(bf16)


def after(value, *others):
    return lax.optimization_barrier((value, *others))[0]


def ring3(value, axis):
    return [value, pp(value, axis, 1), pp(value, axis, 2), pp(value, axis, -1)]


def scatter3(blocks, axis):
    here, behind, far, ahead = blocks
    total = here.astype(f32) + pp(ahead, axis, 1).astype(f32)
    total = total + pp(behind, axis, -1).astype(f32) + pp(far, axis, 2).astype(f32)
    return total.astype(bf16)


def other(value):
    return pp(value, "core", 1)


def both(value):
    return jnp.concatenate([value, other(value)], 0)


def flip(value):
    half = value.shape[0] // 2
    return jnp.concatenate([value[half:], value[:half]], 0)


def dot(left, right):
    return jnp.dot(left, right, preferred_element_type=f32)


def dot_t(left, right):
    return lax.dot_general(left, right, (((1,), (1,)), ((), ())), preferred_element_type=f32)


def t_dot(left, right):
    return lax.dot_general(left, right, (((0,), (0,)), ((), ())), preferred_element_type=f32)


def inverse_root(value):
    return lax.rsqrt(jnp.mean(value * value, -1, keepdims=True) + epsilon)


def layout(lengths):
    ends = jnp.cumsum(lengths, -1)
    places = jnp.arange(ROW, dtype=jnp.int32)
    segment = jnp.sum((places[None, :, None] >= ends[:, None, :]).astype(jnp.int32), -1)
    starts = ends - lengths
    member = segment[:, :, None] == jnp.arange(lengths.shape[-1], dtype=jnp.int32)
    position = places[None, :] - jnp.sum(jnp.where(member, starts[:, None, :], 0), -1)
    allowed = (segment[:, :, None] == segment[:, None, :]) & (
        places[None, :, None] >= places[None, None, :]
    )
    freqs = rope_base ** (-jnp.arange(HEAD_DIM // 2, dtype=f32) * 2.0 / HEAD_DIM)
    turned = position.reshape(-1).astype(f32)[:, None] * jnp.tile(freqs, 4)
    sign = jnp.where(jnp.arange(ROW) % HEAD_DIM < HEAD_DIM // 2, -1.0, 1.0).astype(f32)
    return jnp.where(allowed, 0.0, -1e30).astype(f32), jnp.cos(turned), jnp.sin(turned) * sign


def lanes(rows):
    return lax.broadcasted_iota(jnp.int32, (rows, ROW), 1)


def turn(value, cosine, sine):
    lane = lanes(value.shape[0])
    swapped = jnp.where(lane % HEAD_DIM < HEAD_DIM // 2, pltpu.roll(value, 96, 1), pltpu.roll(value, 32, 1))
    return value * cosine + swapped * sine


def doubled(value):
    low = lanes(value.shape[0]) < HEAD_DIM
    rolled = pltpu.roll(value, HEAD_DIM, 1)
    return jnp.where(low, value, rolled), jnp.where(low, rolled, value)


def split_heads(value):
    low = (lanes(1) < HEAD_DIM).astype(f32).astype(bf16)
    return jnp.concatenate([value * low, value * (1 - low)], 0)


def join_heads(value):
    half = value.shape[0] // 2
    return jnp.where(lanes(half) < HEAD_DIM, value[:half], value[half:])


def attend(query, keys, bias):
    scores = dot_t(query, keys) * HEAD_DIM**-0.5 + bias
    expo = jnp.exp(scores - jnp.max(scores, -1, keepdims=True))
    return expo / jnp.sum(expo, -1, keepdims=True)


def attention_forward_kernel(
    x_ref, gain_ref, *refs
):
    cos_ref, sin_ref, bias_ref, n_ref, q_ref, k_ref, v_ref, o_ref, part_ref, w_qkv, w_out, sems = refs[4:]
    bring_attention(refs[:4], w_qkv, w_out, sems)
    source = x_ref[...].astype(f32)
    n_ref[...] = (source * inverse_root(source) * gain_ref[...]).astype(bf16)
    cosine, sine = cos_ref[...], sin_ref[...]
    for c in range(4):
        wide = dot(n_ref[...], w_qkv[:, 256 * c : 256 * (c + 1)])
        for h in range(2):
            value = wide[:, ROW * h : ROW * (h + 1)]
            if c < 2:
                at = ROW * (2 * c + h)
                q_ref[:, at : at + ROW] = turn(value, cosine, sine).astype(bf16)
                continue
            to = k_ref
            if c == 2:
                value = turn(value, cosine, sine)
            else:
                to = v_ref
            first, second = doubled(value)
            to[:, 256 * h : 256 * h + ROW] = first.astype(bf16)
            to[:, 256 * h + ROW : 256 * (h + 1)] = second.astype(bf16)
    for r in range(2):
        rows = slice(ROW * r, ROW * (r + 1))
        bias = jnp.concatenate([bias_ref[r], bias_ref[r]], 0)
        for g in range(GROUPS):
            cols = slice(ROW * g, ROW * (g + 1))
            prob = attend(split_heads(q_ref[rows, cols]), k_ref[rows, cols], bias).astype(bf16)
            o_ref[rows, cols] = join_heads(dot(prob, v_ref[rows, cols])).astype(bf16)
    part_ref[...] = dot(o_ref[...], w_out[...]).astype(bf16)


def spec(shape, index):
    return pl.BlockSpec(shape, index)


def fixed(shape):
    return pl.BlockSpec(shape, lambda i: (0,) * len(shape))


def shape_of(shape, dtype):
    return jax.ShapeDtypeStruct(shape, dtype)


def params():
    return pltpu.CompilerParams(vmem_limit_bytes=56 * 2**20)


def rows_spec(width):
    return pl.BlockSpec((256, width), lambda i: (i, 0))


def ring_place(s):
    return lax.rem(lax.axis_index("x") - s + 4, 4)


def bring_attention(pieces, w_qkv, w_out, sems):
    @pl.when(pl.program_id(0) == 0)
    def _():
        copies = []
        for s in range(4):
            at = ring_place(s)
            to = w_qkv.at[pl.ds(pl.multiple_of(at * 256, 256), 256)]
            copies.append(pltpu.make_async_copy(pieces[s].at[pl.ds(0, 256)], to, sems.at[2 * s]))
            to = w_out.at[pl.ds(pl.multiple_of(at * ROW, ROW), ROW)]
            copies.append(pltpu.make_async_copy(pieces[s].at[pl.ds(256, ROW)], to, sems.at[2 * s + 1]))
        for copy in copies:
            copy.start()
        for copy in copies:
            copy.wait()


def attention_buffers():
    return [pltpu.VMEM((D, D), bf16), pltpu.VMEM((512, D), bf16), pltpu.SemaphoreType.DMA((8,))]


def attention_forward(x, gain, w_attn, place):
    bias, cosine, sine = place
    return pl.pallas_call(
        attention_forward_kernel,
        grid=(2,),
        in_specs=[
            rows_spec(D), fixed((1, D)), *[afar()] * 4, rows_spec(ROW), rows_spec(ROW),
            spec((2, ROW, ROW), lambda i: (i, 0, 0)),
        ],
        out_specs=[rows_spec(w) for w in (D, 512, 512, 512, 512, D)],
        out_shape=[shape_of((512, w), bf16) for w in (D, 512, 512, 512, 512, D)],
        scratch_shapes=attention_buffers(),
        compiler_params=params(),
        cost_estimate=pl.CostEstimate(flops=1, bytes_accessed=1, transcendentals=0),
        name="attention_forward",
    )(x, gain, *w_attn, cosine, sine, bias)


def weight_copies(weights, buffers, sems):
    own, left, far_gate, far_up, right, down, down_left, down_far, down_far_too, down_right = weights
    gate, up, low = buffers
    sources = [(own.at[0], own.at[1]), (left.at[0], left.at[1]), (far_gate.at[0], far_up.at[0]), (right.at[0], right.at[1])]
    copies = []
    for e in range(OWN):
        low_from = [down.at[e], down_left.at[e], (down_far, down_far_too)[e // 2].at[e % 2], down_right.at[e]]
        group = []
        for s in range(4):
            at = pl.ds(pl.multiple_of(ring_place(s) * 256, 256), 256)
            group.append((sources[e][0].at[s], gate.at[e, at]))
            group.append((sources[e][1].at[s], up.at[e, at]))
            group.append((low_from[s], low.at[e, :, at]))
        copies.append([pltpu.make_async_copy(*pair, sems.at[12 * e + i]) for i, pair in enumerate(group)])
    return copies


def weight_buffers():
    return [
        pltpu.VMEM((OWN, D, FF), bf16),
        pltpu.VMEM((OWN, D, FF), bf16),
        pltpu.VMEM((OWN, FF, D), bf16),
        pltpu.SemaphoreType.DMA((12 * OWN,)),
    ]


def expert_forward_kernel(save, *refs):
    x_ref, part_ref, far_ref, gain_ref, router_ref, chosen_ref = refs[:6]
    weights, refs = refs[6:16], refs[16:]
    if save:
        h_ref, total_ref, n_ref, gates_ref, *stores = refs[:7]
        refs = refs[7:]
    else:
        h_ref, total_ref = refs[:2]
        n_ref, gates_ref = refs[-2:]
        refs = refs[2:-2]
    gate_ref, up_ref, down_ref, sems, acc_ref = refs[:5]
    if save:
        held, out_sems = refs[5:8], refs[8]
    copies = weight_copies(weights, (gate_ref, up_ref, down_ref), sems)
    for group in copies:
        for copy in group:
            copy.start()
    for i in range(4):
        rows = slice(ROW * i, ROW * (i + 1))
        away = slice(ROW * ((i + 2) % 4), ROW * ((i + 2) % 4 + 1))
        hidden = x_ref[rows].astype(f32) + part_ref[rows].astype(f32) + far_ref[away].astype(f32)
        h_ref[rows] = hidden
        normed = (hidden * inverse_root(hidden) * gain_ref[...]).astype(bf16)
        n_ref[rows] = normed
        on = chosen_ref[rows] > 0
        masked = jnp.where(on, dot(normed, router_ref[...]), -1e30)
        raised = jnp.where(on, jnp.exp(masked - jnp.max(masked, -1, keepdims=True)), 0.0)
        gates_ref[rows] = raised / jnp.sum(raised, -1, keepdims=True)
    sent = []
    for e in range(OWN):
        for copy in copies[e]:
            copy.wait()
        cols = slice(FF * e, FF * (e + 1))
        for i in range(2):
            rows = slice(256 * i, 256 * (i + 1))
            gate = jnp.sum(jnp.where(lanes(256) == e, gates_ref[rows], 0.0), -1, keepdims=True)
            a = dot(n_ref[rows], gate_ref[e])
            b = dot(n_ref[rows], up_ref[e])
            acted = (gate * a * lax.logistic(a) * b).astype(bf16)
            if save:
                held[0][rows, cols] = a.astype(bf16)
                held[1][rows, cols] = b.astype(bf16)
                held[2][rows, cols] = acted
            added = dot(acted, down_ref[e])
            if e == 0:
                acc_ref[rows] = added
            elif e < OWN - 1:
                acc_ref[rows] += added
            else:
                total_ref[rows] = (acc_ref[rows] + added).astype(bf16)
        if save:
            for i in range(3):
                copy = pltpu.make_async_copy(held[i].at[:, cols], stores[i].at[:, cols], out_sems.at[3 * e + i])
                copy.start()
                sent.append(copy)
    for copy in sent:
        copy.wait()


def whole():
    return pl.BlockSpec(memory_space=pltpu.VMEM)


def afar():
    return pl.BlockSpec(memory_space=pl.ANY)


def expert_forward(x, part, far, gain, router, chosen, weights, save):
    out_specs = [whole()] * 2
    out_shape = [shape_of((512, D), f32), shape_of((512, D), bf16)]
    scratch = weight_buffers() + [pltpu.VMEM((512, D), f32)]
    if save:
        out_specs += [whole()] * 2 + [afar()] * 3
        out_shape += [shape_of((512, D), bf16), shape_of((512, ROW), f32)] + [shape_of((512, 2048), bf16)] * 3
        scratch += [pltpu.VMEM((512, 2048), bf16)] * 3 + [pltpu.SemaphoreType.DMA((3 * OWN,))]
    else:
        scratch += [pltpu.VMEM((512, D), bf16), pltpu.VMEM((512, ROW), f32)]
    return pl.pallas_call(
        functools.partial(expert_forward_kernel, save),
        in_specs=[whole()] * 6 + [afar()] * 10,
        out_specs=out_specs,
        out_shape=out_shape,
        scratch_shapes=scratch,
        compiler_params=params(),
        cost_estimate=pl.CostEstimate(flops=1, bytes_accessed=1, transcendentals=0),
        name="expert_forward",
    )(x, part, far, gain, router, chosen, *weights)


def expert_backward_kernel(*refs):
    grad_ref, total_ref, far_ref, gates_ref, router_ref, a_ref, b_ref = refs[:7]
    weights = refs[7:17]
    logit_ref, part_ref, *stores = refs[17:21]
    gate_ref, up_ref, down_ref, sems, acc_ref, slope_ref, a_in, b_in, a_out, b_out, row_sems = refs[21:]
    copies = weight_copies(weights, (gate_ref, up_ref, down_ref), sems)
    for e in range(OWN):
        cols = slice(FF * e, FF * (e + 1))
        copies[e].append(pltpu.make_async_copy(a_ref.at[:, cols], a_in.at[:, cols], row_sems.at[4 * e]))
        copies[e].append(pltpu.make_async_copy(b_ref.at[:, cols], b_in.at[:, cols], row_sems.at[4 * e + 1]))
        for copy in copies[e]:
            copy.start()
    inner = []
    for i in range(4):
        rows = slice(ROW * i, ROW * (i + 1))
        away = slice(ROW * ((i + 2) % 4), ROW * ((i + 2) % 4 + 1))
        moe = total_ref[rows].astype(f32) + far_ref[away].astype(f32)
        inner.append(jnp.sum(grad_ref[rows].astype(f32) * moe, -1, keepdims=True))
    inner = [jnp.concatenate(inner[2 * i : 2 * i + 2], 0) for i in range(2)]
    sent = []
    for e in range(OWN):
        for copy in copies[e]:
            copy.wait()
        cols = slice(FF * e, FF * (e + 1))
        for i in range(2):
            rows = slice(256 * i, 256 * (i + 1))
            mine = lanes(256) == e
            gate = jnp.sum(jnp.where(mine, gates_ref[rows], 0.0), -1, keepdims=True)
            wide = dot_t(grad_ref[rows], down_ref[e])
            a, b = a_in[rows, cols].astype(f32), b_in[rows, cols].astype(f32)
            sigma = lax.logistic(a)
            raised = wide * a * sigma
            slope = jnp.where(mine, gate * (jnp.sum(raised * b, -1, keepdims=True) - inner[i]), 0.0)
            a_out[rows, cols] = (gate * wide * b * sigma * (1.0 + a * (1.0 - sigma))).astype(bf16)
            b_out[rows, cols] = (gate * raised).astype(bf16)
            added = dot_t(a_out[rows, cols], gate_ref[e]) + dot_t(b_out[rows, cols], up_ref[e])
            if e == 0:
                slope_ref[rows] = slope
                acc_ref[rows] = added
            elif e < OWN - 1:
                slope_ref[rows] += slope
                acc_ref[rows] += added
            else:
                logit_ref[rows] = (slope_ref[rows] + slope).astype(bf16)
                added = added + dot_t(logit_ref[rows], router_ref[...])
                part_ref[rows] = (acc_ref[rows] + added).astype(bf16)
        for i, held in enumerate((a_out, b_out)):
            copy = pltpu.make_async_copy(held.at[:, cols], stores[i].at[:, cols], row_sems.at[4 * e + 2 + i])
            copy.start()
            sent.append(copy)
    for copy in sent:
        copy.wait()


def expert_backward(grad, total, far, gates, router, a, b, weights):
    return pl.pallas_call(
        expert_backward_kernel,
        in_specs=[whole()] * 5 + [afar()] * 12,
        out_specs=[whole()] * 2 + [afar()] * 2,
        out_shape=[shape_of((512, ROW), bf16), shape_of((512, D), bf16)] + [shape_of((512, 2048), bf16)] * 2,
        scratch_shapes=weight_buffers()
        + [pltpu.VMEM((512, D), f32), pltpu.VMEM((512, ROW), f32)]
        + [pltpu.VMEM((512, 2048), bf16)] * 4
        + [pltpu.SemaphoreType.DMA((4 * OWN,))],
        compiler_params=params(),
        cost_estimate=pl.CostEstimate(flops=1, bytes_accessed=1, transcendentals=0),
        name="expert_backward",
    )(grad, total, far, gates, router, a, b, *weights)


def expert_grads_kernel(n_ref, a_ref, b_ref, *refs):
    *outs, turned_ref = refs

    @pl.when(pl.program_id(0) == 0)
    def _():
        turned_ref[...] = n_ref[...].T

    for i in range(4):
        rows = slice(256 * i, 256 * (i + 1))
        if len(outs) == 1:
            out, at = outs[0].at[0], rows
        else:
            out, at = outs[i // 2], slice(256 * (i % 2), 256 * (i % 2 + 1))
        out[at, :FF] = dot(turned_ref[rows], a_ref[...]).astype(bf16)
        out[at, FF:] = dot(turned_ref[rows], b_ref[...]).astype(bf16)


def expert_grads(normed, gate_grad, up_grad, far):
    if far:
        slots = spec((512, FF), lambda e: (0, 2))
        out_specs, out_shape = [fixed((512, D))] * 2, [shape_of((512, D), bf16)] * 2
    else:
        slots = spec((512, FF), lambda e: (0, e + e // 2))
        out_specs, out_shape = spec((1, D, D), lambda e: (e, 0, 0)), shape_of((3, D, D), bf16)
    return pl.pallas_call(
        expert_grads_kernel,
        grid=(1 if far else 3,),
        in_specs=[fixed((512, D)), slots, slots],
        out_specs=out_specs,
        out_shape=out_shape,
        scratch_shapes=[pltpu.VMEM((D, 512), bf16)],
        compiler_params=params(),
        cost_estimate=pl.CostEstimate(flops=1, bytes_accessed=1, transcendentals=0),
        name="expert_grads",
    )(normed, gate_grad, up_grad)


def attention_grads_kernel(n_ref, qkv_ref, o_ref, a_ref, small_ref, out_ref):
    out_ref[0, :256] = t_dot(n_ref[...], qkv_ref[...]).astype(bf16)
    out_ref[0, 256:384] = t_dot(o_ref[...], a_ref[...]).astype(bf16)
    out_ref[0, 384:] = jnp.concatenate([small_ref[...], jnp.zeros((32, D - 256), bf16)], -1)


def attention_grads(normed, qkv_grad, mixed, grad_attn, small):
    return pl.pallas_call(
        attention_grads_kernel,
        grid=(4,),
        in_specs=[
            spec((512, 256), lambda s: (0, s)), fixed((512, D)), spec((512, ROW), lambda s: (0, s)),
            fixed((512, D)), spec((32, 256), lambda s: (0, s)),
        ],
        out_specs=spec((1, 416, D), lambda s: (s, 0, 0)),
        out_shape=shape_of((4, 416, D), bf16),
        compiler_params=params(),
        cost_estimate=pl.CostEstimate(flops=1, bytes_accessed=1, transcendentals=0),
        name="attention_grads",
    )(normed, qkv_grad, mixed, grad_attn, small)


def sides(near, far):
    first = lax.axis_index("core") == 0
    near, far = near.astype(f32), far.astype(f32)
    return jnp.where(first, near, far), jnp.where(first, far, near)


def spread_pair_kernel(pair, pair_far, gate, up):
    for y in range(4):
        for c, side in enumerate(sides(pair[y], pair_far[y])):
            gate[:, 4 * c + y, :] = side[:, :FF]
            up[:, 4 * c + y, :] = side[:, FF:]


def spread_pair(packed, theirs):
    return pl.pallas_call(
        spread_pair_kernel,
        grid=(4,),
        in_specs=[spec((4, 64, D), lambda i: (0, i, 0))] * 2,
        out_specs=[spec((64, 8, FF), lambda i: (i, 0, 0))] * 2,
        out_shape=[shape_of((256, 8, FF), f32)] * 2,
        compiler_params=params(),
        cost_estimate=pl.CostEstimate(flops=1, bytes_accessed=1, transcendentals=0),
        name="spread_pair",
    )(packed, theirs)


def spread_rest_kernel(low, low_far, attn, attn_far, mix, mix_far, down, query, key, value, out):
    for y in range(4):
        for c, side in enumerate(sides(low[y], low_far[y])):
            down[4 * c + y] = side
    for c, side in enumerate(sides(mix[0], mix_far[0])):
        out[c] = side
    near, far = sides(attn[0], attn_far[0])
    below = lanes(64) < HEAD_DIM
    for s in range(4):
        query[:, 256 * s : 256 * s + ROW] = near[:, ROW * s : ROW * (s + 1)]
        query[:, 256 * s + ROW : 256 * (s + 1)] = far[:, ROW * s : ROW * (s + 1)]
    for to, base in ((key, 512), (value, 768)):
        for h in range(2):
            a = near[:, base + ROW * h : base + ROW * (h + 1)]
            b = far[:, base + ROW * h : base + ROW * (h + 1)]
            to[:, 256 * h : 256 * h + ROW] = jnp.where(below, a, pltpu.roll(b, HEAD_DIM, 1))
            to[:, 256 * h + ROW : 256 * (h + 1)] = jnp.where(below, pltpu.roll(a, HEAD_DIM, 1), b)


def spread_rest(packed, theirs):
    specs = [
        spec((4, ROW, 256), lambda i: (0, 0, i)),
        spec((1, 64, D), lambda i: (i, 2, 0)),
        spec((1, 32, D), lambda i: (i, 6, 0)),
    ]
    return pl.pallas_call(
        spread_rest_kernel,
        grid=(4,),
        in_specs=[item for item in specs for _ in range(2)],
        out_specs=[
            spec((8, ROW, 256), lambda i: (0, i, 0)),
            spec((64, D), lambda i: (i, 0)),
            spec((64, 512), lambda i: (i, 0)),
            spec((64, 512), lambda i: (i, 0)),
            spec((2, 32, D), lambda i: (0, i, 0)),
        ],
        out_shape=[
            shape_of(shape, f32) for shape in ((8, FF, 256), (256, D), (256, 512), (256, 512), (2, ROW, D))
        ],
        compiler_params=params(),
        cost_estimate=pl.CostEstimate(flops=1, bytes_accessed=1, transcendentals=0),
        name="spread_rest",
    )(*[packed, theirs] * 3)


def norm_backward(grad_normed, value, gain):
    scale = inverse_root(value)
    scaled = grad_normed * gain
    change = scale * scaled - value * scale**3 * jnp.mean(value * scaled, -1, keepdims=True)
    return change, jnp.sum(grad_normed * value * scale, 0, keepdims=True)


def attention_backward_kernel(
    grad_ref, h_ref, near_ref, far_ref, gain_ref, *refs
):
    q_ref, k_ref, v_ref, cos_ref, sin_ref, bias_ref = refs[4:10]
    dh_ref, da_ref, dqkv_ref, part_ref, gain_grad_ref, do_ref, w_qkv, w_out, sems = refs[10:]
    bring_attention(refs[:4], w_qkv, w_out, sems)
    change, gain_grad = norm_backward(
        near_ref[...].astype(f32) + far_ref[...].astype(f32), h_ref[...], gain_ref[...]
    )

    @pl.when(pl.program_id(0) == 0)
    def _():
        gain_grad_ref[...] = gain_grad

    grad_hidden = grad_ref[...].astype(f32) + change
    dh_ref[...] = grad_hidden
    da_ref[...] = grad_hidden.astype(bf16)
    do_ref[...] = dot_t(da_ref[...], w_out[...]).astype(bf16)
    for r in range(2):
        rows = slice(ROW * r, ROW * (r + 1))
        bias = jnp.concatenate([bias_ref[r], bias_ref[r]], 0)
        cosine, sine = cos_ref[rows], -sin_ref[rows]
        key_grads, value_grads = [], []
        for g in range(GROUPS):
            cols = slice(ROW * g, ROW * (g + 1))
            query = split_heads(q_ref[rows, cols])
            keys = k_ref[rows, cols]
            prob = attend(query, keys, bias)
            grad_mixed = split_heads(do_ref[rows, cols])
            grad_prob = dot_t(grad_mixed, v_ref[rows, cols])
            value_grads.append(t_dot(prob.astype(bf16), grad_mixed))
            inner = jnp.sum(prob * grad_prob, -1, keepdims=True)
            grad_scores = (prob * (grad_prob - inner) * HEAD_DIM**-0.5).astype(bf16)
            dqkv_ref[rows, cols] = turn(join_heads(dot(grad_scores, keys)), cosine, sine).astype(bf16)
            key_grads.append(t_dot(grad_scores, query))
        for h in range(2):
            low = lanes(ROW) < HEAD_DIM
            pair = [v + pltpu.roll(v, HEAD_DIM, 1) for v in key_grads[2 * h : 2 * h + 2]]
            at = 512 + ROW * h
            dqkv_ref[rows, at : at + ROW] = turn(jnp.where(low, *pair), cosine, sine).astype(bf16)
            pair = [v + pltpu.roll(v, HEAD_DIM, 1) for v in value_grads[2 * h : 2 * h + 2]]
            at = 768 + ROW * h
            dqkv_ref[rows, at : at + ROW] = jnp.where(low, *pair).astype(bf16)
    part_ref[...] = dot_t(dqkv_ref[...], w_qkv[...]).astype(bf16)


def attention_backward(grad, hidden, near, far, gain, w_attn, query, keys, values, place):
    bias, cosine, sine = place
    return pl.pallas_call(
        attention_backward_kernel,
        grid=(2,),
        in_specs=[
            rows_spec(D), rows_spec(D), rows_spec(D), pl.BlockSpec((256, D), lambda i: (1 - i, 0)),
            fixed((1, D)), *[afar()] * 4,
            rows_spec(512), rows_spec(512), rows_spec(512), rows_spec(ROW), rows_spec(ROW),
            spec((2, ROW, ROW), lambda i: (i, 0, 0)),
        ],
        out_specs=[rows_spec(D)] * 4 + [fixed((1, D))],
        out_shape=[shape_of((512, D), f32)] + [shape_of((512, D), bf16)] * 3 + [shape_of((1, D), f32)],
        scratch_shapes=[pltpu.VMEM((256, 512), bf16)] + attention_buffers(),
        compiler_params=params(),
        cost_estimate=pl.CostEstimate(flops=1, bytes_accessed=1, transcendentals=0),
        name="attention_backward",
    )(grad, hidden, near, far, gain, *w_attn, query, keys, values, cosine, sine, bias)


def local(
    inputs, cotangent, lengths, expert_ids, gain_attn, w_query, w_key, w_value, w_out,
    gain_ffn, w_router, w_gate, w_up, w_down,
):
    section = lax.axis_index("section")
    x_at, y_at, core = lax.axis_index("x"), lax.axis_index("y"), lax.axis_index("core")

    expert = core * OWN + y_at
    pair = jnp.stack(
        [lax.dynamic_index_in_dim(w_gate[0], expert, 1, False), lax.dynamic_index_in_dim(w_up[0], expert, 1, False)], 0
    )
    pair = jnp.stack(ring3(pair, "x"), 1)
    q_own = lax.dynamic_index_in_dim(w_query[0].reshape(256, 4, 2, 128), core, 2, False).reshape(256, 512)
    k_own = lax.dynamic_index_in_dim(w_key[0].reshape(256, 4, 2, 64), core, 2, False).reshape(256, 256)
    v_own = lax.dynamic_index_in_dim(w_value[0].reshape(256, 4, 2, 64), core, 2, False).reshape(256, 256)
    out_own = lax.dynamic_slice_in_dim(w_out[0], core * 128, 128, 0)
    small = jnp.concatenate([gain_attn[0][None], gain_ffn[0][None], w_router[0].T], 0)
    small = jnp.pad(small, ((0, 6), (0, D - 256)))
    attn_own = jnp.concatenate([jnp.concatenate([q_own, k_own, v_own], -1), out_own, small], 0)
    down_own = involute(lax.dynamic_slice_in_dim(w_down[0], core * OWN, OWN, 0), 0, y_at)
    attn_own, down_own, pair = lax.optimization_barrier((attn_own, down_own, pair))
    left, right = pp(pair, "y", 1), pp(pair, "y", -1)
    attn_all = ring3(attn_own, "x")
    down_left, down_right = pp(down_own, "x", 1), pp(down_own, "x", -1)
    far_gate, far_up = pp(left[:1], "y", 1), pp(right[1:], "y", -1)
    start = both(inputs.reshape(256, D))
    down_far, down_far_too = pp(down_left[:2], "x", 1), pp(down_right[2:], "x", -1)
    weights = (pair, left, far_gate, far_up, right, down_own, down_left, down_far, down_far_too, down_right)
    small_all = involute(jnp.concatenate([v[384:394, :256] for v in attn_all], -1), 1, x_at)
    gain_one = small_all[:1].astype(f32)
    gain_two = small_all[1:2].astype(f32)

    marks = jnp.concatenate(
        [expert_ids[0].reshape(256, 4), jnp.broadcast_to(lengths, (2, 128, 4)).reshape(256, 4)], -1
    )
    marks = both(marks)
    ids = marks[:, :4]
    place = layout(marks[:, 4:].reshape(4, 128, 4)[:, 0])
    near = core * OWN + (y_at - jnp.arange(OWN)) % OWN
    slots = jnp.concatenate([near, (near + OWN) % 8, jnp.full((ROW - 8,), -1)])
    chosen = jnp.sum((ids[:, :, None] == slots).astype(f32), 1)
    router = t_dot(small_all[2:10], (jnp.arange(8)[:, None] == slots).astype(bf16)).astype(bf16)

    x = start
    for phase in range(2):
        normed, query, keys, values, mixed, part = attention_forward(x, gain_one, attn_all, place)
        hidden, total, *record = expert_forward(
            x, part, other(part), gain_two, router, chosen, weights, phase == 1
        )
        total_far = other(total)
        moe = total[:256].astype(f32) + total_far[256:].astype(f32)
        own_out = (hidden[:256] + moe).astype(bf16)
        if phase == 0:
            received = lax.ppermute(own_out, "section", [(0, 1)])
            x = jnp.where(section == 0, start, both(received))

    normed_two, gates, gate_in, up_in, acted = record
    grad = both(cotangent.reshape(256, D))
    first = grad
    source = x[:256].astype(f32)
    for phase in range(2):
        logit_grad, part, gate_grad, up_grad = expert_backward(
            grad, total, total_far, gates, router, gate_in, up_in, weights
        )
        if phase == 1:
            far_grads = expert_grads(normed_two, gate_grad, up_grad, True)
            far_sent = (pp(far_grads[0], "y", 1), pp(far_grads[1], "y", -1))
            near_grads = expert_grads(after(normed_two, *far_grads), gate_grad, up_grad, False)
            part = after(part, near_grads)
        grad_hidden, grad_attn, qkv_grad, part, gain_two_grad = attention_backward(
            grad, hidden, part, other(part), gain_two, attn_all, query, keys, values, place
        )
        if phase == 1:
            far_sent = (after(far_sent[0], part), after(far_sent[1], part))
            ahead = jnp.concatenate([plus(near_grads[2, :512], far_sent[0]), near_grads[2, 512:]], 0)
            behind = jnp.concatenate([near_grads[1, :512], plus(near_grads[1, 512:], far_sent[1])], 0)
            part = after(part, ahead, behind)
            qkv_grad = after(qkv_grad, ahead, behind)
            ahead, behind = pp(ahead, "y", 1), pp(behind, "y", -1)
        far = other(part)
        grad_normed = part[:256].astype(f32) + far[256:].astype(f32)
        change, gain_one_grad = norm_backward(grad_normed, source, gain_one)
        own_grad = (grad_hidden[:256] + change).astype(bf16)
        if phase == 0:
            received = lax.ppermute(own_grad, "section", [(1, 0)])
            grad = jnp.where(section == 1, first, both(received))

    down_grad = t_dot(after(acted, *far_grads), grad).astype(bf16).reshape(OWN, FF, D)
    down_sum = lax.psum_scatter(down_grad, "x", scatter_dimension=2, tiled=True)
    router_grad = t_dot(normed_two, logit_grad)[:, :OWN]
    placed = jnp.zeros((8, D), f32)
    placed = lax.dynamic_update_slice_in_dim(placed, involute(router_grad.T, 0, y_at), core * OWN, 0)
    small_grads = jnp.concatenate([gain_one_grad, gain_two_grad, placed, jnp.zeros((22, D), f32)], 0)
    attn_grads = attention_grads(normed, qkv_grad, mixed, grad_attn, small_grads.astype(bf16))
    attn_sum = lax.psum_scatter(attn_grads, "x", scatter_dimension=0)
    down_sum = after(down_sum, attn_grads)
    down_sum = plus(down_sum, pp(down_sum, "zh", 1))

    ahead, behind = after(ahead, down_sum), after(behind, down_sum)
    pair_sum = (near_grads[0].astype(f32) + ahead.astype(f32) + behind.astype(f32)).astype(bf16)
    pair_sum = lax.psum_scatter(pair_sum.reshape(4, 256, D), "x", scatter_dimension=0)
    attn_sum = plus(attn_sum, pp(attn_sum, "zh", 1))

    parts = [(attn_sum[:256], 64), (attn_sum[256:384], 32), (attn_sum[384:], 8)]
    parts = [(involute(part, 0, y_at), size) for part, size in parts]

    def rest(e):
        down = jnp.concatenate([down_sum[e, ROW * i : ROW * (i + 1)] for i in range(4)], -1)
        return jnp.concatenate([down] + [part[size * e : size * (e + 1)] for part, size in parts], 0)

    rest_blocks = [rest(e) for e in range(OWN)]
    rest_sum = scatter3(rest_blocks, "y")
    pair_sum = plus(pair_sum, pp(pair_sum, "zh", 1))
    pair_all = lax.all_gather(pair_sum, "y")
    rest_all = lax.all_gather(rest_sum, "y")
    rest_far = other(rest_all)
    pair_far = other(pair_all)
    grad_gate, grad_up = spread_pair(pair_all, pair_far)
    grad_down, grad_query, grad_key, grad_value, grad_out = spread_rest(rest_all, rest_far)
    grad_out = grad_out.reshape(256, D)
    small_sum = rest_all[:2, 224:, :256].astype(f32) + rest_far[:2, 224:, :256].astype(f32)
    small_sum = small_sum.reshape(16, 256)

    outputs = own_out.reshape(2, ROW, D)
    input_grads = own_grad.reshape(2, ROW, D)
    return (
        outputs[None],
        input_grads[None],
        small_sum[0][None],
        grad_query[None],
        grad_key[None],
        grad_value[None],
        grad_out[None],
        small_sum[1][None],
        small_sum[2:10].T[None],
        grad_gate[None],
        grad_up[None],
        grad_down[None],
    )


def solution(mesh):
    fine = Mesh(mesh.devices.reshape(2, 4, 2, 2, 4), ("section", "y", "zh", "core", "x"))
    rows = ("y", "zh", "core", "x")
    return jax.shard_map(
        local,
        mesh=fine,
        in_specs=(
            P(None, rows, None),
            P(None, rows, None),
            P(None, rows, None),
            P("section", None, rows, None),
            P("section", "x"),
            P("section", "x", None),
            P("section", "x", None),
            P("section", "x", None),
            P("section", "x", None),
            P("section", "x"),
            P("section", "x", None),
            P("section", "x", None, None),
            P("section", "x", None, None),
            P("section", None, None, "x"),
        ),
        out_specs=(
            P("section", None, rows, None),
            P("section", None, rows, None),
            P("section", "x"),
            P("section", "x", None),
            P("section", "x", None),
            P("section", "x", None),
            P("section", "x", None),
            P("section", "x"),
            P("section", "x", None),
            P("section", "x", None, None),
            P("section", "x", None, None),
            P("section", None, None, "x"),
        ),
        check_vma=False,
    )
```

```python
import functools

import jax
import jax.numpy as jnp
from jax import lax
from jax.experimental import pallas as pl
from jax.experimental.pallas import tpu as pltpu
from jax.sharding import Mesh, PartitionSpec as P

D = 1024
HEAD_DIM = 64
GROUPS = 4
FF = 512
OWN = 4
ROW = 128
epsilon = 1e-05
rope_base = 10000.0
bf16 = jnp.bfloat16
f32 = jnp.float32


def pp(value, axis, step):
    count = lax.axis_size(axis)
    return lax.ppermute(value, axis, [(i, (i + step) % count) for i in range(count)])


def involute(value, dim, index):
    size = value.shape[dim] // 4
    blocks = [lax.slice_in_dim(value, i * size, (i + 1) * size, axis=dim) for i in (3, 2, 1, 0)]
    double = jnp.concatenate(blocks + blocks[:3], dim)
    return lax.dynamic_slice_in_dim(double, (3 - index) * size, 4 * size, dim)


def plus(first, second):
    return (first.astype(f32) + second.astype(f32)).astype(bf16)


def after(value, *others):
    return lax.optimization_barrier((value, *others))[0]


def ring3(value, axis):
    return [value, pp(value, axis, 1), pp(value, axis, 2), pp(value, axis, -1)]


def scatter3(blocks, axis):
    here, behind, far, ahead = blocks
    total = here.astype(f32) + pp(ahead, axis, 1).astype(f32)
    total = total + pp(behind, axis, -1).astype(f32) + pp(far, axis, 2).astype(f32)
    return total.astype(bf16)


def other(value):
    return pp(value, "core", 1)


def both(value):
    return jnp.concatenate([value, other(value)], 0)


def flip(value):
    half = value.shape[0] // 2
    return jnp.concatenate([value[half:], value[:half]], 0)


def dot(left, right):
    return jnp.dot(left, right, preferred_element_type=f32)


def dot_t(left, right):
    return lax.dot_general(left, right, (((1,), (1,)), ((), ())), preferred_element_type=f32)


def t_dot(left, right):
    return lax.dot_general(left, right, (((0,), (0,)), ((), ())), preferred_element_type=f32)


def inverse_root(value):
    return lax.rsqrt(jnp.mean(value * value, -1, keepdims=True) + epsilon)


def layout(lengths):
    ends = jnp.cumsum(lengths, -1)
    places = jnp.arange(ROW, dtype=jnp.int32)
    segment = jnp.sum((places[None, :, None] >= ends[:, None, :]).astype(jnp.int32), -1)
    starts = ends - lengths
    member = segment[:, :, None] == jnp.arange(lengths.shape[-1], dtype=jnp.int32)
    position = places[None, :] - jnp.sum(jnp.where(member, starts[:, None, :], 0), -1)
    allowed = (segment[:, :, None] == segment[:, None, :]) & (
        places[None, :, None] >= places[None, None, :]
    )
    freqs = rope_base ** (-jnp.arange(HEAD_DIM // 2, dtype=f32) * 2.0 / HEAD_DIM)
    turned = position.reshape(-1).astype(f32)[:, None] * jnp.tile(freqs, 4)
    sign = jnp.where(jnp.arange(ROW) % HEAD_DIM < HEAD_DIM // 2, -1.0, 1.0).astype(f32)
    return jnp.where(allowed, 0.0, -1e30).astype(f32), jnp.cos(turned), jnp.sin(turned) * sign


def lanes(rows):
    return lax.broadcasted_iota(jnp.int32, (rows, ROW), 1)


def turn(value, cosine, sine):
    lane = lanes(value.shape[0])
    swapped = jnp.where(lane % HEAD_DIM < HEAD_DIM // 2, pltpu.roll(value, 96, 1), pltpu.roll(value, 32, 1))
    return value * cosine + swapped * sine


def doubled(value):
    low = lanes(value.shape[0]) < HEAD_DIM
    rolled = pltpu.roll(value, HEAD_DIM, 1)
    return jnp.where(low, value, rolled), jnp.where(low, rolled, value)


def split_heads(value):
    low = (lanes(1) < HEAD_DIM).astype(f32).astype(bf16)
    return jnp.concatenate([value * low, value * (1 - low)], 0)


def join_heads(value):
    half = value.shape[0] // 2
    return jnp.where(lanes(half) < HEAD_DIM, value[:half], value[half:])


def attend(query, keys, bias):
    scores = dot_t(query, keys) * HEAD_DIM**-0.5 + bias
    expo = jnp.exp(scores - jnp.max(scores, -1, keepdims=True))
    return expo / jnp.sum(expo, -1, keepdims=True)


def attention_forward_kernel(
    x_ref, gain_ref, *refs
):
    cos_ref, sin_ref, bias_ref, n_ref, q_ref, k_ref, v_ref, o_ref, part_ref, w_qkv, w_out, sems = refs[4:]
    bring_attention(refs[:4], w_qkv, w_out, sems)
    source = x_ref[...].astype(f32)
    n_ref[...] = (source * inverse_root(source) * gain_ref[...]).astype(bf16)
    cosine, sine = cos_ref[...], sin_ref[...]
    for c in range(4):
        wide = dot(n_ref[...], w_qkv[:, 256 * c : 256 * (c + 1)])
        for h in range(2):
            value = wide[:, ROW * h : ROW * (h + 1)]
            if c < 2:
                at = ROW * (2 * c + h)
                q_ref[:, at : at + ROW] = turn(value, cosine, sine).astype(bf16)
                continue
            to = k_ref
            if c == 2:
                value = turn(value, cosine, sine)
            else:
                to = v_ref
            first, second = doubled(value)
            to[:, 256 * h : 256 * h + ROW] = first.astype(bf16)
            to[:, 256 * h + ROW : 256 * (h + 1)] = second.astype(bf16)
    for r in range(2):
        rows = slice(ROW * r, ROW * (r + 1))
        bias = jnp.concatenate([bias_ref[r], bias_ref[r]], 0)
        for g in range(GROUPS):
            cols = slice(ROW * g, ROW * (g + 1))
            prob = attend(split_heads(q_ref[rows, cols]), k_ref[rows, cols], bias).astype(bf16)
            o_ref[rows, cols] = join_heads(dot(prob, v_ref[rows, cols])).astype(bf16)
    part_ref[...] = dot(o_ref[...], w_out[...]).astype(bf16)


def spec(shape, index):
    return pl.BlockSpec(shape, index)


def fixed(shape):
    return pl.BlockSpec(shape, lambda i: (0,) * len(shape))


def shape_of(shape, dtype):
    return jax.ShapeDtypeStruct(shape, dtype)


def params():
    return pltpu.CompilerParams(vmem_limit_bytes=56 * 2**20)


def rows_spec(width):
    return pl.BlockSpec((256, width), lambda i: (i, 0))


def ring_place(s):
    return lax.rem(lax.axis_index("x") - s + 4, 4)


def bring_attention(pieces, w_qkv, w_out, sems):
    @pl.when(pl.program_id(0) == 0)
    def _():
        copies = []
        for s in range(4):
            at = ring_place(s)
            to = w_qkv.at[pl.ds(pl.multiple_of(at * 256, 256), 256)]
            copies.append(pltpu.make_async_copy(pieces[s].at[pl.ds(0, 256)], to, sems.at[2 * s]))
            to = w_out.at[pl.ds(pl.multiple_of(at * ROW, ROW), ROW)]
            copies.append(pltpu.make_async_copy(pieces[s].at[pl.ds(256, ROW)], to, sems.at[2 * s + 1]))
        for copy in copies:
            copy.start()
        for copy in copies:
            copy.wait()


def attention_buffers():
    return [pltpu.VMEM((D, D), bf16), pltpu.VMEM((512, D), bf16), pltpu.SemaphoreType.DMA((8,))]


def attention_forward(x, gain, w_attn, place):
    bias, cosine, sine = place
    return pl.pallas_call(
        attention_forward_kernel,
        grid=(2,),
        in_specs=[
            rows_spec(D), fixed((1, D)), *[afar()] * 4, rows_spec(ROW), rows_spec(ROW),
            spec((2, ROW, ROW), lambda i: (i, 0, 0)),
        ],
        out_specs=[rows_spec(w) for w in (D, 512, 512, 512, 512, D)],
        out_shape=[shape_of((512, w), bf16) for w in (D, 512, 512, 512, 512, D)],
        scratch_shapes=attention_buffers(),
        compiler_params=params(),
        cost_estimate=pl.CostEstimate(flops=1, bytes_accessed=1, transcendentals=0),
        name="attention_forward",
    )(x, gain, *w_attn, cosine, sine, bias)


def weight_copies(weights, buffers, sems):
    own, left, far_gate, far_up, right, down, down_left, down_far, down_far_too, down_right = weights
    gate, up, low = buffers
    sources = [(own.at[0], own.at[1]), (left.at[0], left.at[1]), (far_gate.at[0], far_up.at[0]), (right.at[0], right.at[1])]
    copies = []
    for e in range(OWN):
        low_from = [down.at[e], down_left.at[e], (down_far, down_far_too)[e // 2].at[e % 2], down_right.at[e]]
        group = []
        for s in range(4):
            at = pl.ds(pl.multiple_of(ring_place(s) * 256, 256), 256)
            group.append((sources[e][0].at[s], gate.at[e, at]))
            group.append((sources[e][1].at[s], up.at[e, at]))
            group.append((low_from[s], low.at[e, :, at]))
        copies.append([pltpu.make_async_copy(*pair, sems.at[12 * e + i]) for i, pair in enumerate(group)])
    return copies


def weight_buffers():
    return [
        pltpu.VMEM((OWN, D, FF), bf16),
        pltpu.VMEM((OWN, D, FF), bf16),
        pltpu.VMEM((OWN, FF, D), bf16),
        pltpu.SemaphoreType.DMA((12 * OWN,)),
    ]


def expert_forward_kernel(save, *refs):
    x_ref, part_ref, far_ref, gain_ref, router_ref, chosen_ref = refs[:6]
    weights, refs = refs[6:16], refs[16:]
    if save:
        h_ref, total_ref, n_ref, gates_ref, *stores = refs[:7]
        refs = refs[7:]
    else:
        h_ref, total_ref = refs[:2]
        n_ref, gates_ref = refs[-2:]
        refs = refs[2:-2]
    gate_ref, up_ref, down_ref, sems, acc_ref = refs[:5]
    if save:
        held, out_sems = refs[5:8], refs[8]
    copies = weight_copies(weights, (gate_ref, up_ref, down_ref), sems)
    for group in copies:
        for copy in group:
            copy.start()
    for i in range(4):
        rows = slice(ROW * i, ROW * (i + 1))
        away = slice(ROW * ((i + 2) % 4), ROW * ((i + 2) % 4 + 1))
        hidden = x_ref[rows].astype(f32) + part_ref[rows].astype(f32) + far_ref[away].astype(f32)
        h_ref[rows] = hidden
        normed = (hidden * inverse_root(hidden) * gain_ref[...]).astype(bf16)
        n_ref[rows] = normed
        on = chosen_ref[rows] > 0
        masked = jnp.where(on, dot(normed, router_ref[...]), -1e30)
        raised = jnp.where(on, jnp.exp(masked - jnp.max(masked, -1, keepdims=True)), 0.0)
        gates_ref[rows] = raised / jnp.sum(raised, -1, keepdims=True)
    sent = []
    for e in range(OWN):
        for copy in copies[e]:
            copy.wait()
        cols = slice(FF * e, FF * (e + 1))
        for i in range(2):
            rows = slice(256 * i, 256 * (i + 1))
            gate = jnp.sum(jnp.where(lanes(256) == e, gates_ref[rows], 0.0), -1, keepdims=True)
            a = dot(n_ref[rows], gate_ref[e])
            b = dot(n_ref[rows], up_ref[e])
            acted = (gate * a * lax.logistic(a) * b).astype(bf16)
            if save:
                held[0][rows, cols] = a.astype(bf16)
                held[1][rows, cols] = b.astype(bf16)
                held[2][rows, cols] = acted
            added = dot(acted, down_ref[e])
            if e == 0:
                acc_ref[rows] = added
            elif e < OWN - 1:
                acc_ref[rows] += added
            else:
                total_ref[rows] = (acc_ref[rows] + added).astype(bf16)
        if save:
            for i in range(3):
                copy = pltpu.make_async_copy(held[i].at[:, cols], stores[i].at[:, cols], out_sems.at[3 * e + i])
                copy.start()
                sent.append(copy)
    for copy in sent:
        copy.wait()


def whole():
    return pl.BlockSpec(memory_space=pltpu.VMEM)


def afar():
    return pl.BlockSpec(memory_space=pl.ANY)


def expert_forward(x, part, far, gain, router, chosen, weights, save):
    out_specs = [whole()] * 2
    out_shape = [shape_of((512, D), f32), shape_of((512, D), bf16)]
    scratch = weight_buffers() + [pltpu.VMEM((512, D), f32)]
    if save:
        out_specs += [whole()] * 2 + [afar()] * 3
        out_shape += [shape_of((512, D), bf16), shape_of((512, ROW), f32)] + [shape_of((512, 2048), bf16)] * 3
        scratch += [pltpu.VMEM((512, 2048), bf16)] * 3 + [pltpu.SemaphoreType.DMA((3 * OWN,))]
    else:
        scratch += [pltpu.VMEM((512, D), bf16), pltpu.VMEM((512, ROW), f32)]
    return pl.pallas_call(
        functools.partial(expert_forward_kernel, save),
        in_specs=[whole()] * 6 + [afar()] * 10,
        out_specs=out_specs,
        out_shape=out_shape,
        scratch_shapes=scratch,
        compiler_params=params(),
        cost_estimate=pl.CostEstimate(flops=1, bytes_accessed=1, transcendentals=0),
        name="expert_forward",
    )(x, part, far, gain, router, chosen, *weights)


def expert_backward_kernel(*refs):
    grad_ref, total_ref, far_ref, gates_ref, router_ref, a_ref, b_ref = refs[:7]
    weights = refs[7:17]
    logit_ref, part_ref, *stores = refs[17:21]
    gate_ref, up_ref, down_ref, sems, acc_ref, slope_ref, a_in, b_in, a_out, b_out, row_sems = refs[21:]
    copies = weight_copies(weights, (gate_ref, up_ref, down_ref), sems)
    for e in range(OWN):
        cols = slice(FF * e, FF * (e + 1))
        copies[e].append(pltpu.make_async_copy(a_ref.at[:, cols], a_in.at[:, cols], row_sems.at[4 * e]))
        copies[e].append(pltpu.make_async_copy(b_ref.at[:, cols], b_in.at[:, cols], row_sems.at[4 * e + 1]))
        for copy in copies[e]:
            copy.start()
    inner = []
    for i in range(4):
        rows = slice(ROW * i, ROW * (i + 1))
        away = slice(ROW * ((i + 2) % 4), ROW * ((i + 2) % 4 + 1))
        moe = total_ref[rows].astype(f32) + far_ref[away].astype(f32)
        inner.append(jnp.sum(grad_ref[rows].astype(f32) * moe, -1, keepdims=True))
    inner = [jnp.concatenate(inner[2 * i : 2 * i + 2], 0) for i in range(2)]
    sent = []
    for e in range(OWN):
        for copy in copies[e]:
            copy.wait()
        cols = slice(FF * e, FF * (e + 1))
        for i in range(2):
            rows = slice(256 * i, 256 * (i + 1))
            mine = lanes(256) == e
            gate = jnp.sum(jnp.where(mine, gates_ref[rows], 0.0), -1, keepdims=True)
            wide = dot_t(grad_ref[rows], down_ref[e])
            a, b = a_in[rows, cols].astype(f32), b_in[rows, cols].astype(f32)
            sigma = lax.logistic(a)
            raised = wide * a * sigma
            slope = jnp.where(mine, gate * (jnp.sum(raised * b, -1, keepdims=True) - inner[i]), 0.0)
            a_out[rows, cols] = (gate * wide * b * sigma * (1.0 + a * (1.0 - sigma))).astype(bf16)
            b_out[rows, cols] = (gate * raised).astype(bf16)
            added = dot_t(a_out[rows, cols], gate_ref[e]) + dot_t(b_out[rows, cols], up_ref[e])
            if e == 0:
                slope_ref[rows] = slope
                acc_ref[rows] = added
            elif e < OWN - 1:
                slope_ref[rows] += slope
                acc_ref[rows] += added
            else:
                logit_ref[rows] = (slope_ref[rows] + slope).astype(bf16)
                added = added + dot_t(logit_ref[rows], router_ref[...])
                part_ref[rows] = (acc_ref[rows] + added).astype(bf16)
        for i, held in enumerate((a_out, b_out)):
            copy = pltpu.make_async_copy(held.at[:, cols], stores[i].at[:, cols], row_sems.at[4 * e + 2 + i])
            copy.start()
            sent.append(copy)
    for copy in sent:
        copy.wait()


def expert_backward(grad, total, far, gates, router, a, b, weights):
    return pl.pallas_call(
        expert_backward_kernel,
        in_specs=[whole()] * 5 + [afar()] * 12,
        out_specs=[whole()] * 2 + [afar()] * 2,
        out_shape=[shape_of((512, ROW), bf16), shape_of((512, D), bf16)] + [shape_of((512, 2048), bf16)] * 2,
        scratch_shapes=weight_buffers()
        + [pltpu.VMEM((512, D), f32), pltpu.VMEM((512, ROW), f32)]
        + [pltpu.VMEM((512, 2048), bf16)] * 4
        + [pltpu.SemaphoreType.DMA((4 * OWN,))],
        compiler_params=params(),
        cost_estimate=pl.CostEstimate(flops=1, bytes_accessed=1, transcendentals=0),
        name="expert_backward",
    )(grad, total, far, gates, router, a, b, *weights)


def expert_grads_kernel(n_ref, a_ref, b_ref, *refs):
    *outs, turned_ref = refs

    @pl.when(pl.program_id(0) == 0)
    def _():
        turned_ref[...] = n_ref[...].T

    for i in range(4):
        rows = slice(256 * i, 256 * (i + 1))
        if len(outs) == 1:
            out, at = outs[0].at[0], rows
        else:
            out, at = outs[i // 2], slice(256 * (i % 2), 256 * (i % 2 + 1))
        out[at, :FF] = dot(turned_ref[rows], a_ref[...]).astype(bf16)
        out[at, FF:] = dot(turned_ref[rows], b_ref[...]).astype(bf16)


def expert_grads(normed, gate_grad, up_grad, far):
    if far:
        slots = spec((512, FF), lambda e: (0, 2))
        out_specs, out_shape = [fixed((512, D))] * 2, [shape_of((512, D), bf16)] * 2
    else:
        slots = spec((512, FF), lambda e: (0, e + e // 2))
        out_specs, out_shape = spec((1, D, D), lambda e: (e, 0, 0)), shape_of((3, D, D), bf16)
    return pl.pallas_call(
        expert_grads_kernel,
        grid=(1 if far else 3,),
        in_specs=[fixed((512, D)), slots, slots],
        out_specs=out_specs,
        out_shape=out_shape,
        scratch_shapes=[pltpu.VMEM((D, 512), bf16)],
        compiler_params=params(),
        cost_estimate=pl.CostEstimate(flops=1, bytes_accessed=1, transcendentals=0),
        name="expert_grads",
    )(normed, gate_grad, up_grad)


def attention_grads_kernel(n_ref, qkv_ref, o_ref, a_ref, small_ref, out_ref):
    out_ref[0, :256] = t_dot(n_ref[...], qkv_ref[...]).astype(bf16)
    out_ref[0, 256:384] = t_dot(o_ref[...], a_ref[...]).astype(bf16)
    out_ref[0, 384:] = jnp.concatenate([small_ref[...], jnp.zeros((32, D - 256), bf16)], -1)


def attention_grads(normed, qkv_grad, mixed, grad_attn, small):
    return pl.pallas_call(
        attention_grads_kernel,
        grid=(4,),
        in_specs=[
            spec((512, 256), lambda s: (0, s)), fixed((512, D)), spec((512, ROW), lambda s: (0, s)),
            fixed((512, D)), spec((32, 256), lambda s: (0, s)),
        ],
        out_specs=spec((1, 416, D), lambda s: (s, 0, 0)),
        out_shape=shape_of((4, 416, D), bf16),
        compiler_params=params(),
        cost_estimate=pl.CostEstimate(flops=1, bytes_accessed=1, transcendentals=0),
        name="attention_grads",
    )(normed, qkv_grad, mixed, grad_attn, small)


def sides(near, far):
    first = lax.axis_index("core") == 0
    near, far = near.astype(f32), far.astype(f32)
    return jnp.where(first, near, far), jnp.where(first, far, near)


def spread_pair_kernel(pair, pair_far, gate, up):
    for y in range(4):
        for c, side in enumerate(sides(pair[y], pair_far[y])):
            gate[:, 4 * c + y, :] = side[:, :FF]
            up[:, 4 * c + y, :] = side[:, FF:]


def spread_pair(packed, theirs):
    return pl.pallas_call(
        spread_pair_kernel,
        grid=(4,),
        in_specs=[spec((4, 64, D), lambda i: (0, i, 0))] * 2,
        out_specs=[spec((64, 8, FF), lambda i: (i, 0, 0))] * 2,
        out_shape=[shape_of((256, 8, FF), f32)] * 2,
        compiler_params=params(),
        cost_estimate=pl.CostEstimate(flops=1, bytes_accessed=1, transcendentals=0),
        name="spread_pair",
    )(packed, theirs)


def spread_rest_kernel(low, low_far, attn, attn_far, mix, mix_far, down, query, key, value, out):
    for y in range(4):
        for c, side in enumerate(sides(low[y], low_far[y])):
            down[4 * c + y] = side
    for c, side in enumerate(sides(mix[0], mix_far[0])):
        out[c] = side
    near, far = sides(attn[0], attn_far[0])
    below = lanes(64) < HEAD_DIM
    for s in range(4):
        query[:, 256 * s : 256 * s + ROW] = near[:, ROW * s : ROW * (s + 1)]
        query[:, 256 * s + ROW : 256 * (s + 1)] = far[:, ROW * s : ROW * (s + 1)]
    for to, base in ((key, 512), (value, 768)):
        for h in range(2):
            a = near[:, base + ROW * h : base + ROW * (h + 1)]
            b = far[:, base + ROW * h : base + ROW * (h + 1)]
            to[:, 256 * h : 256 * h + ROW] = jnp.where(below, a, pltpu.roll(b, HEAD_DIM, 1))
            to[:, 256 * h + ROW : 256 * (h + 1)] = jnp.where(below, pltpu.roll(a, HEAD_DIM, 1), b)


def spread_rest(packed, theirs):
    specs = [
        spec((4, ROW, 256), lambda i: (0, 0, i)),
        spec((1, 64, D), lambda i: (i, 2, 0)),
        spec((1, 32, D), lambda i: (i, 6, 0)),
    ]
    return pl.pallas_call(
        spread_rest_kernel,
        grid=(4,),
        in_specs=[item for item in specs for _ in range(2)],
        out_specs=[
            spec((8, ROW, 256), lambda i: (0, i, 0)),
            spec((64, D), lambda i: (i, 0)),
            spec((64, 512), lambda i: (i, 0)),
            spec((64, 512), lambda i: (i, 0)),
            spec((2, 32, D), lambda i: (0, i, 0)),
        ],
        out_shape=[
            shape_of(shape, f32) for shape in ((8, FF, 256), (256, D), (256, 512), (256, 512), (2, ROW, D))
        ],
        compiler_params=params(),
        cost_estimate=pl.CostEstimate(flops=1, bytes_accessed=1, transcendentals=0),
        name="spread_rest",
    )(*[packed, theirs] * 3)


def norm_backward(grad_normed, value, gain):
    scale = inverse_root(value)
    scaled = grad_normed * gain
    change = scale * scaled - value * scale**3 * jnp.mean(value * scaled, -1, keepdims=True)
    return change, jnp.sum(grad_normed * value * scale, 0, keepdims=True)


def attention_backward_kernel(
    grad_ref, h_ref, near_ref, far_ref, gain_ref, *refs
):
    q_ref, k_ref, v_ref, cos_ref, sin_ref, bias_ref = refs[4:10]
    dh_ref, da_ref, dqkv_ref, part_ref, gain_grad_ref, do_ref, w_qkv, w_out, sems = refs[10:]
    bring_attention(refs[:4], w_qkv, w_out, sems)
    change, gain_grad = norm_backward(
        near_ref[...].astype(f32) + far_ref[...].astype(f32), h_ref[...], gain_ref[...]
    )

    @pl.when(pl.program_id(0) == 0)
    def _():
        gain_grad_ref[...] = gain_grad

    grad_hidden = grad_ref[...].astype(f32) + change
    dh_ref[...] = grad_hidden
    da_ref[...] = grad_hidden.astype(bf16)
    do_ref[...] = dot_t(da_ref[...], w_out[...]).astype(bf16)
    for r in range(2):
        rows = slice(ROW * r, ROW * (r + 1))
        bias = jnp.concatenate([bias_ref[r], bias_ref[r]], 0)
        cosine, sine = cos_ref[rows], -sin_ref[rows]
        key_grads, value_grads = [], []
        for g in range(GROUPS):
            cols = slice(ROW * g, ROW * (g + 1))
            query = split_heads(q_ref[rows, cols])
            keys = k_ref[rows, cols]
            prob = attend(query, keys, bias)
            grad_mixed = split_heads(do_ref[rows, cols])
            grad_prob = dot_t(grad_mixed, v_ref[rows, cols])
            value_grads.append(t_dot(prob.astype(bf16), grad_mixed))
            inner = jnp.sum(prob * grad_prob, -1, keepdims=True)
            grad_scores = (prob * (grad_prob - inner) * HEAD_DIM**-0.5).astype(bf16)
            dqkv_ref[rows, cols] = turn(join_heads(dot(grad_scores, keys)), cosine, sine).astype(bf16)
            key_grads.append(t_dot(grad_scores, query))
        for h in range(2):
            low = lanes(ROW) < HEAD_DIM
            pair = [v + pltpu.roll(v, HEAD_DIM, 1) for v in key_grads[2 * h : 2 * h + 2]]
            at = 512 + ROW * h
            dqkv_ref[rows, at : at + ROW] = turn(jnp.where(low, *pair), cosine, sine).astype(bf16)
            pair = [v + pltpu.roll(v, HEAD_DIM, 1) for v in value_grads[2 * h : 2 * h + 2]]
            at = 768 + ROW * h
            dqkv_ref[rows, at : at + ROW] = jnp.where(low, *pair).astype(bf16)
    part_ref[...] = dot_t(dqkv_ref[...], w_qkv[...]).astype(bf16)


def attention_backward(grad, hidden, near, far, gain, w_attn, query, keys, values, place):
    bias, cosine, sine = place
    return pl.pallas_call(
        attention_backward_kernel,
        grid=(2,),
        in_specs=[
            rows_spec(D), rows_spec(D), rows_spec(D), pl.BlockSpec((256, D), lambda i: (1 - i, 0)),
            fixed((1, D)), *[afar()] * 4,
            rows_spec(512), rows_spec(512), rows_spec(512), rows_spec(ROW), rows_spec(ROW),
            spec((2, ROW, ROW), lambda i: (i, 0, 0)),
        ],
        out_specs=[rows_spec(D)] * 4 + [fixed((1, D))],
        out_shape=[shape_of((512, D), f32)] + [shape_of((512, D), bf16)] * 3 + [shape_of((1, D), f32)],
        scratch_shapes=[pltpu.VMEM((256, 512), bf16)] + attention_buffers(),
        compiler_params=params(),
        cost_estimate=pl.CostEstimate(flops=1, bytes_accessed=1, transcendentals=0),
        name="attention_backward",
    )(grad, hidden, near, far, gain, *w_attn, query, keys, values, cosine, sine, bias)


def local(
    inputs, cotangent, lengths, expert_ids, gain_attn, w_query, w_key, w_value, w_out,
    gain_ffn, w_router, w_gate, w_up, w_down,
):
    section = lax.axis_index("section")
    x_at, y_at, core = lax.axis_index("x"), lax.axis_index("y"), lax.axis_index("core")

    expert = core * OWN + y_at
    pair = jnp.stack(
        [lax.dynamic_index_in_dim(w_gate[0], expert, 1, False), lax.dynamic_index_in_dim(w_up[0], expert, 1, False)], 0
    )
    pair = jnp.stack(ring3(pair, "x"), 1)
    q_own = lax.dynamic_index_in_dim(w_query[0].reshape(256, 4, 2, 128), core, 2, False).reshape(256, 512)
    k_own = lax.dynamic_index_in_dim(w_key[0].reshape(256, 4, 2, 64), core, 2, False).reshape(256, 256)
    v_own = lax.dynamic_index_in_dim(w_value[0].reshape(256, 4, 2, 64), core, 2, False).reshape(256, 256)
    out_own = lax.dynamic_slice_in_dim(w_out[0], core * 128, 128, 0)
    small = jnp.concatenate([gain_attn[0][None], gain_ffn[0][None], w_router[0].T], 0)
    small = jnp.pad(small, ((0, 6), (0, D - 256)))
    attn_own = jnp.concatenate([jnp.concatenate([q_own, k_own, v_own], -1), out_own, small], 0)
    down_own = involute(lax.dynamic_slice_in_dim(w_down[0], core * OWN, OWN, 0), 0, y_at)
    attn_own, down_own, pair = lax.optimization_barrier((attn_own, down_own, pair))
    left, right = pp(pair, "y", 1), pp(pair, "y", -1)
    attn_all = ring3(attn_own, "x")
    down_left, down_right = pp(down_own, "x", 1), pp(down_own, "x", -1)
    far_gate, far_up = pp(left[:1], "y", 1), pp(right[1:], "y", -1)
    start = both(inputs.reshape(256, D))
    down_far, down_far_too = pp(down_left[:2], "x", 1), pp(down_right[2:], "x", -1)
    weights = (pair, left, far_gate, far_up, right, down_own, down_left, down_far, down_far_too, down_right)
    small_all = involute(jnp.concatenate([v[384:394, :256] for v in attn_all], -1), 1, x_at)
    gain_one = small_all[:1].astype(f32)
    gain_two = small_all[1:2].astype(f32)

    marks = jnp.concatenate(
        [expert_ids[0].reshape(256, 4), jnp.broadcast_to(lengths, (2, 128, 4)).reshape(256, 4)], -1
    )
    marks = both(marks)
    ids = marks[:, :4]
    place = layout(marks[:, 4:].reshape(4, 128, 4)[:, 0])
    near = core * OWN + (y_at - jnp.arange(OWN)) % OWN
    slots = jnp.concatenate([near, (near + OWN) % 8, jnp.full((ROW - 8,), -1)])
    chosen = jnp.sum((ids[:, :, None] == slots).astype(f32), 1)
    router = t_dot(small_all[2:10], (jnp.arange(8)[:, None] == slots).astype(bf16)).astype(bf16)

    x = start
    for phase in range(2):
        normed, query, keys, values, mixed, part = attention_forward(x, gain_one, attn_all, place)
        hidden, total, *record = expert_forward(
            x, part, other(part), gain_two, router, chosen, weights, phase == 1
        )
        total_far = other(total)
        moe = total[:256].astype(f32) + total_far[256:].astype(f32)
        own_out = (hidden[:256] + moe).astype(bf16)
        if phase == 0:
            received = lax.ppermute(own_out, "section", [(0, 1)])
            x = jnp.where(section == 0, start, both(received))

    normed_two, gates, gate_in, up_in, acted = record
    grad = both(cotangent.reshape(256, D))
    first = grad
    source = x[:256].astype(f32)
    for phase in range(2):
        logit_grad, part, gate_grad, up_grad = expert_backward(
            grad, total, total_far, gates, router, gate_in, up_in, weights
        )
        if phase == 1:
            far_grads = expert_grads(normed_two, gate_grad, up_grad, True)
            far_sent = (pp(far_grads[0], "y", 1), pp(far_grads[1], "y", -1))
            near_grads = expert_grads(after(normed_two, *far_grads), gate_grad, up_grad, False)
            part = after(part, near_grads)
        grad_hidden, grad_attn, qkv_grad, part, gain_two_grad = attention_backward(
            grad, hidden, part, other(part), gain_two, attn_all, query, keys, values, place
        )
        if phase == 1:
            far_sent = (after(far_sent[0], part), after(far_sent[1], part))
            ahead = jnp.concatenate([plus(near_grads[2, :512], far_sent[0]), near_grads[2, 512:]], 0)
            behind = jnp.concatenate([near_grads[1, :512], plus(near_grads[1, 512:], far_sent[1])], 0)
            part = after(part, ahead, behind)
            qkv_grad = after(qkv_grad, ahead, behind)
            ahead, behind = pp(ahead, "y", 1), pp(behind, "y", -1)
        far = other(part)
        grad_normed = part[:256].astype(f32) + far[256:].astype(f32)
        change, gain_one_grad = norm_backward(grad_normed, source, gain_one)
        own_grad = (grad_hidden[:256] + change).astype(bf16)
        if phase == 0:
            received = lax.ppermute(own_grad, "section", [(1, 0)])
            grad = jnp.where(section == 1, first, both(received))

    down_grad = t_dot(after(acted, *far_grads), grad).astype(bf16).reshape(OWN, FF, D)
    down_sum = lax.psum_scatter(down_grad, "x", scatter_dimension=2, tiled=True)
    router_grad = t_dot(normed_two, logit_grad)[:, :OWN]
    placed = jnp.zeros((8, D), f32)
    placed = lax.dynamic_update_slice_in_dim(placed, involute(router_grad.T, 0, y_at), core * OWN, 0)
    small_grads = jnp.concatenate([gain_one_grad, gain_two_grad, placed, jnp.zeros((22, D), f32)], 0)
    attn_grads = attention_grads(normed, qkv_grad, mixed, grad_attn, small_grads.astype(bf16))
    attn_sum = lax.psum_scatter(attn_grads, "x", scatter_dimension=0)
    down_sum = after(down_sum, attn_grads)
    down_sum = plus(down_sum, pp(down_sum, "zh", 1))

    ahead, behind = after(ahead, down_sum), after(behind, down_sum)
    pair_sum = (near_grads[0].astype(f32) + ahead.astype(f32) + behind.astype(f32)).astype(bf16)
    pair_sum = lax.psum_scatter(pair_sum.reshape(4, 256, D), "x", scatter_dimension=0)
    attn_sum = plus(attn_sum, pp(attn_sum, "zh", 1))

    parts = [(attn_sum[:256], 64), (attn_sum[256:384], 32), (attn_sum[384:], 8)]
    parts = [(involute(part, 0, y_at), size) for part, size in parts]

    def rest(e):
        down = jnp.concatenate([down_sum[e, ROW * i : ROW * (i + 1)] for i in range(4)], -1)
        return jnp.concatenate([down] + [part[size * e : size * (e + 1)] for part, size in parts], 0)

    rest_blocks = [rest(e) for e in range(OWN)]
    rest_sum = scatter3(rest_blocks, "y")
    pair_sum = plus(pair_sum, pp(pair_sum, "zh", 1))
    pair_all = ring3(pair_sum, "y")
    rest_all = lax.all_gather(rest_sum, "y")
    rest_far = other(rest_all)
    pair_all = involute(jnp.stack(pair_all, 0), 0, y_at)
    pair_far = other(pair_all)
    grad_gate, grad_up = spread_pair(pair_all, pair_far)
    grad_down, grad_query, grad_key, grad_value, grad_out = spread_rest(rest_all, rest_far)
    grad_out = grad_out.reshape(256, D)
    small_sum = rest_all[:2, 224:, :256].astype(f32) + rest_far[:2, 224:, :256].astype(f32)
    small_sum = small_sum.reshape(16, 256)

    outputs = own_out.reshape(2, ROW, D)
    input_grads = own_grad.reshape(2, ROW, D)
    return (
        outputs[None],
        input_grads[None],
        small_sum[0][None],
        grad_query[None],
        grad_key[None],
        grad_value[None],
        grad_out[None],
        small_sum[1][None],
        small_sum[2:10].T[None],
        grad_gate[None],
        grad_up[None],
        grad_down[None],
    )


def solution(mesh):
    fine = Mesh(mesh.devices.reshape(2, 4, 2, 2, 4), ("section", "y", "zh", "core", "x"))
    rows = ("y", "zh", "core", "x")
    return jax.shard_map(
        local,
        mesh=fine,
        in_specs=(
            P(None, rows, None),
            P(None, rows, None),
            P(None, rows, None),
            P("section", None, rows, None),
            P("section", "x"),
            P("section", "x", None),
            P("section", "x", None),
            P("section", "x", None),
            P("section", "x", None),
            P("section", "x"),
            P("section", "x", None),
            P("section", "x", None, None),
            P("section", "x", None, None),
            P("section", None, None, "x"),
        ),
        out_specs=(
            P("section", None, rows, None),
            P("section", None, rows, None),
            P("section", "x"),
            P("section", "x", None),
            P("section", "x", None),
            P("section", "x", None),
            P("section", "x", None),
            P("section", "x"),
            P("section", "x", None),
            P("section", "x", None, None),
            P("section", "x", None, None),
            P("section", None, None, "x"),
        ),
        check_vma=False,
    )
```
